128 devices in a mesh: dp: 16 (over y, x_lo, core), fsdp: 8 (over z, x_hi).
Axes of the slice: x: 4 (x_hi: 2, x_lo: 2; x = x_hi * 2 + x_lo), y: 4, z: 4, core: 2. Of those that a mesh axis runs over, the one named last changes fastest.
Arguments:
- grads: bfloat16 [16, 16, 8, 512, 512], P('dp', None, 'fsdp'), may hold values from -250 to 250
- left_factor: float32 [16, 8, 512, 512], P('dp', 'fsdp'), may hold values from -1 to 8
- right_factor: float32 [16, 8, 512, 512], P('dp', 'fsdp'), may hold values from -1 to 8
- left_basis: bfloat16 [16, 8, 512, 512], P('dp', 'fsdp'), may hold values from -1 to 2
- right_basis: bfloat16 [16, 8, 512, 512], P('dp', 'fsdp'), may hold values from -1 to 2
- first_moment: bfloat16 [16, 8, 512, 512], P('dp', 'fsdp'), may hold values from -0.59765625 to 0.59765625
- second_moment: float32 [16, 8, 512, 512], P('dp', 'fsdp'), may hold values from 0.001 to 0.03
- parameters: bfloat16 [16, 8, 512, 512], P('dp', 'fsdp'), may hold values from -6 to 6
- rotation: int32 [8], P('fsdp'), may hold values from 0 to 15
Outputs:
- parameters_out: bfloat16 [16, 8, 512, 512], P(None, 'fsdp')
- left_out: float32 [16, 8, 512, 512], P('dp', 'fsdp')
- right_out: float32 [16, 8, 512, 512], P('dp', 'fsdp')
- left_basis_out: bfloat16 [16, 8, 512, 512], P('dp', 'fsdp')
- right_basis_out: bfloat16 [16, 8, 512, 512], P('dp', 'fsdp')
- first_out: bfloat16 [16, 8, 512, 512], P('dp', 'fsdp')
- second_out: float32 [16, 8, 512, 512], P('dp', 'fsdp')
The draws below stay inside these ranges and needn't reach their ends.
All inputs are finite; a program needn't handle non-finite values.
Results may differ from the reference program's by a relative error of at most 0.038.
Values may be sent and summed in bfloat16 or wider, within the bound.
A program may use at most 128 MiB of HBM per device.

```python
import math
import jax
import jax.numpy as jnp
from jax import lax

BLOCK = 512
ITERS = 2
NEWTON = 3
REPLICAS = 16
ROWS = 16
COLS = 8


def draw_grads(key, part):
    key = jax.random.fold_in(key, 11)
    row_key = jax.random.fold_in(key, 0)
    col_key = jax.random.fold_in(key, 1)
    noise_key = jax.random.fold_in(key, 3)
    shape = (ROWS, COLS, BLOCK, BLOCK)
    row_scale = jnp.exp(jax.random.uniform(row_key, (BLOCK, 1), jnp.float32, 0.0, math.log(10.0) / 2))
    col_scale = jnp.exp(jax.random.uniform(col_key, (1, BLOCK), jnp.float32, 0.0, math.log(10.0) / 2))
    position = jnp.arange(ROWS * COLS, dtype=jnp.float32).reshape(ROWS, COLS, 1, 1) / max(ROWS * COLS - 1, 1)
    rising = jnp.sqrt(1.0 + 4.0 * position)

    def one_replica(index):
        own = jnp.clip(jax.random.normal(jax.random.fold_in(noise_key, index), shape, jnp.float32), -4.0, 4.0)
        return (own * rising * row_scale * col_scale).astype(jnp.bfloat16)
    return lax.map(one_replica, jnp.arange(REPLICAS, dtype=jnp.int32))


def positive_blocks(raw_values, scale_key):
    symmetric = (raw_values + jnp.swapaxes(raw_values, -1, -2)) * (0.5 / math.sqrt(2.0 * BLOCK))
    identity = jnp.eye(BLOCK, dtype=jnp.float32)
    scales = jnp.exp(jax.random.uniform(scale_key, (ROWS, COLS, BLOCK), jnp.float32, 0.0, math.log(1.7)))
    return scales[..., :, None] * (2.0 * identity + symmetric) * scales[..., None, :]


def draw_left_factor(key, part):
    key = jax.random.fold_in(key, 21)
    noise_key, scale_key = jax.random.split(key)
    shape = (ROWS, COLS, BLOCK, BLOCK)
    raw_values = jnp.clip(jax.random.normal(noise_key, shape, jnp.float32), -3.0, 3.0)
    return positive_blocks(raw_values, scale_key)


def draw_right_factor(key, part):
    key = jax.random.fold_in(key, 22)
    noise_key, scale_key = jax.random.split(key)
    shape = (ROWS, COLS, BLOCK, BLOCK)
    raw_values = jnp.clip(jax.random.normal(noise_key, shape, jnp.float32), -3.0, 3.0)
    return positive_blocks(raw_values, scale_key)


def near_identity(raw_values):
    identity = jnp.eye(BLOCK, dtype=jnp.float32)
    return (identity + 0.25 * raw_values / math.sqrt(BLOCK)).astype(jnp.bfloat16)


def draw_left_basis(key, part):
    key = jax.random.fold_in(key, 31)
    shape = (ROWS, COLS, BLOCK, BLOCK)
    raw_values = jnp.clip(jax.random.normal(key, shape, jnp.float32), -3.0, 3.0)
    return near_identity(raw_values)


def draw_right_basis(key, part):
    key = jax.random.fold_in(key, 32)
    shape = (ROWS, COLS, BLOCK, BLOCK)
    raw_values = jnp.clip(jax.random.normal(key, shape, jnp.float32), -3.0, 3.0)
    return near_identity(raw_values)


def plant(values, stream_key, smallest, top_value):
    extent = values.shape
    spot = [jax.random.randint(jax.random.fold_in(stream_key, axis), (), 0, extent[axis]) for axis in range(len(extent))]
    values = values.at[tuple(spot)].set(smallest)
    longest = extent.index(max(extent))
    spot[longest] = (spot[longest] + 1) % extent[longest]
    return values.at[tuple(spot)].set(top_value)


def block_scale(key, dims, cuts, low, top_value):
    def one(axis_at, shards_of):
        steps = jax.random.uniform(jax.random.fold_in(jax.random.fold_in(key, 6), axis_at), (shards_of,), jnp.float32, low / len(cuts), top_value / len(cuts))
        return jnp.repeat(jnp.exp(steps), dims[axis_at] // shards_of).reshape((-1,) + (1,) * (len(dims) - axis_at - 1))

    level = one(*cuts[0])
    for cut in cuts[1:]:
        level = level * one(*cut)
    return level


def normal_values(stream_key, extent, scale, limit, cuts=(), held_as=jnp.bfloat16):
    result = jax.random.normal(stream_key, extent, jnp.float32) * scale
    if len(cuts) > 0:
        result = block_scale(stream_key, extent, cuts, -0.22, 0.18) * result
    return jnp.clip(result, min=-limit, max=limit).astype(held_as)


def setup_inputs(seed: int = 0) -> dict:
    key_list = jax.random.split(jax.random.key(seed), 10)
    return {
        "grads": draw_grads(jax.random.fold_in(key_list[9], 71), 0),
        "left_factor": draw_left_factor(jax.random.fold_in(key_list[9], 71), 0),
        "right_factor": draw_right_factor(jax.random.fold_in(key_list[9], 71), 0),
        "left_basis": draw_left_basis(jax.random.fold_in(key_list[9], 71), 0),
        "right_basis": draw_right_basis(jax.random.fold_in(key_list[9], 71), 0),
        "first_moment": normal_values(key_list[5], (ROWS, COLS, BLOCK, BLOCK), 0.1, 0.59765625, ((0, 16), (1, 8))),
        "second_moment": jnp.clip(jnp.exp(math.log(0.03) - 3.4011973 * jax.random.uniform(key_list[6], (ROWS, COLS, BLOCK, BLOCK), jnp.float32) ** block_scale(key_list[6], (ROWS, COLS, BLOCK, BLOCK), ((0, 16), (1, 8)), -0.2, 0.2)), 0.001, 0.03),
        "parameters": normal_values(key_list[7], (ROWS, COLS, BLOCK, BLOCK), 1.0, 6.0, ((0, 16), (1, 8))),
        "rotation": plant(jax.random.randint(key_list[8], (COLS,), 0, ROWS), jax.random.fold_in(key_list[8], 1), 0, ROWS - 1).astype(jnp.int32),
    }


BETA_MOMENT = 0.95
BETA_SECOND = 0.95
BETA_FACTOR = 0.95
STEP_RATE = 0.05
CLIP_RMS = 0.3
TINY = 1e-08

def orthonormal(factor, basis_start):
    factor_low = factor.astype(jnp.bfloat16)
    basis_now = basis_start
    identity = jnp.eye(factor.shape[0], dtype=jnp.float32)
    for repeat in range(ITERS):
        image_cols = jnp.dot(factor_low, basis_now, preferred_element_type=jnp.float32)
        magnitude = jnp.abs(image_cols)
        bound = jnp.sqrt(jnp.max(lax.optimization_barrier(jnp.sum(magnitude, axis=0))) * jnp.max(lax.optimization_barrier(jnp.sum(magnitude, axis=1)))) + 1e-06
        iterate = image_cols / bound
        for newton_step in range(NEWTON):
            gram_matrix = jnp.dot(iterate.T, iterate, precision=lax.Precision.HIGHEST, preferred_element_type=jnp.float32)
            iterate = jnp.dot(iterate, 1.5 * identity - 0.5 * gram_matrix, precision=lax.Precision.HIGHEST, preferred_element_type=jnp.float32)
        basis_now = iterate.astype(jnp.bfloat16)
    return basis_now

def block_step(grad_mean, clip_factor, left_old, right_old, left_basis_old, right_basis_old, first_old, second_old, param_old):
    grad_low = grad_mean.astype(jnp.bfloat16)
    half_left = jnp.dot(left_basis_old.T, grad_low, preferred_element_type=jnp.float32).astype(jnp.bfloat16)
    rotated = clip_factor * jnp.dot(half_left, right_basis_old, preferred_element_type=jnp.float32)
    moment = BETA_MOMENT * first_old.astype(jnp.float32) + (1.0 - BETA_MOMENT) * rotated
    second_new = BETA_SECOND * second_old + (1.0 - BETA_SECOND) * rotated * rotated
    direction = (moment / (jnp.sqrt(second_new) + TINY)).astype(jnp.bfloat16)
    half_back = jnp.dot(left_basis_old, direction, preferred_element_type=jnp.float32).astype(jnp.bfloat16)
    update = jnp.dot(half_back, right_basis_old.T, preferred_element_type=jnp.float32)
    param_new = (param_old.astype(jnp.float32) - STEP_RATE * update).astype(jnp.bfloat16)
    squared_clip = clip_factor * clip_factor
    left_new = BETA_FACTOR * left_old + (1.0 - BETA_FACTOR) * squared_clip * jnp.dot(grad_low, grad_low.T, preferred_element_type=jnp.float32)
    right_new = BETA_FACTOR * right_old + (1.0 - BETA_FACTOR) * squared_clip * jnp.dot(grad_low.T, grad_low, preferred_element_type=jnp.float32)
    left_turned = orthonormal(left_new, left_basis_old)
    right_turned = orthonormal(right_new, right_basis_old)
    left_turn = jnp.dot(left_turned.T, left_basis_old, preferred_element_type=jnp.float32).astype(jnp.bfloat16)
    right_turn = jnp.dot(right_basis_old.T, right_turned, preferred_element_type=jnp.float32).astype(jnp.bfloat16)
    half_turned = jnp.dot(left_turn, moment.astype(jnp.bfloat16), preferred_element_type=jnp.float32).astype(jnp.bfloat16)
    first_new = jnp.dot(half_turned, right_turn, preferred_element_type=jnp.float32).astype(jnp.bfloat16)
    return (param_new, left_new, right_new, left_turned, right_turned, first_new, second_new)

def reference(grads, left_factor, right_factor, left_basis, right_basis, first_moment, second_moment, parameters, rotation):
    grad_mean = lax.optimization_barrier(jnp.sum(grads, axis=0, dtype=jnp.float32)) * (1.0 / REPLICAS)
    square_sum = jnp.sum(grad_mean * grad_mean)
    clip_factor = jnp.minimum(1.0, CLIP_RMS * math.sqrt(grad_mean.size) / jnp.sqrt(square_sum + 1e-06))
    side = grad_mean.shape[-1]
    blocks = ROWS * COLS

    def flatten(values):
        return values.reshape(blocks, side, side)

    def one_block(items):
        return block_step(items[0], clip_factor, items[1], items[2], items[3], items[4], items[5], items[6], items[7])
    results = lax.map(one_block, (flatten(grad_mean), flatten(left_factor), flatten(right_factor), flatten(left_basis), flatten(right_basis), flatten(first_moment), flatten(second_moment), flatten(parameters)))
    shaped = [values.reshape(ROWS, COLS, side, side) for values in results]
    index_table = (jnp.arange(ROWS, dtype=jnp.int32)[:, None] - rotation[None, :].astype(jnp.int32)) % ROWS

    def relocate(values):
        pieces = [jnp.take(values[:, column], index_table[:, column], axis=0) for column in range(COLS)]
        return jnp.stack(pieces, axis=1)
    return (shaped[0], relocate(shaped[1]), relocate(shaped[2]), relocate(shaped[3]), relocate(shaped[4]), relocate(shaped[5]), relocate(shaped[6]))
```

```python
import math

import jax
import jax.numpy as jnp
from jax import lax
from jax.experimental import pallas as pl
from jax.experimental.pallas import tpu as pltpu
from jax.sharding import PartitionSpec as P

ITERS = 2
NEWTON = 3
SIDE = 512
REPLICAS = 16
COLUMNS = 8
CHUNK = SIDE // REPLICAS

BETA_MOMENT = 0.95
BETA_SECOND = 0.95
BETA_FACTOR = 0.95
STEP_RATE = 0.05
CLIP_RMS = 0.3
TINY = 1e-08

Y_ROWS = 208
X_ROWS = SIDE - Y_ROWS
YS = pl.ds(0, Y_ROWS)
XS = pl.ds(Y_ROWS, X_ROWS)

MESH = pl.DeviceIdType.MESH
BF = jnp.bfloat16
F32 = jnp.float32


def place():
    me = lax.axis_index("dp")
    return me, me // 4, me // 2 % 2, me % 2


def index_of(y, x, core):
    return y % 4 * 4 + x % 2 * 2 + core % 2


def remote(src, dst, send, recv, **where):
    return pltpu.make_async_remote_copy(
        src_ref=src, dst_ref=dst, send_sem=send, recv_sem=recv, device_id=where, device_id_type=MESH
    )


def greet_replicas(barrier, me):
    def greet(step, carry):
        pl.semaphore_signal(
            barrier, inc=1, device_id={"dp": (me + step) % REPLICAS}, device_id_type=MESH
        )
        return carry

    lax.fori_loop(1, REPLICAS, greet, 0)


def reduce_kernel(
    grads,
    low_out,
    total_out,
    own,
    twin,
    x_in,
    y_in,
    y_late,
    x_late,
    tile,
    tile2,
    local_sem,
    core_send,
    core_recv,
    send,
    recv,
    ring_send,
    ring_recv,
    column_send,
    column_recv,
):
    me, y, x, core = place()
    column = lax.axis_index("fsdp")
    barrier = pltpu.get_barrier_semaphore()
    greet_replicas(barrier, me)

    def greet_column(step, carry):
        pl.semaphore_signal(
            barrier, inc=1, device_id={"fsdp": (column + step) % COLUMNS}, device_id_type=MESH
        )
        return carry

    lax.fori_loop(1, COLUMNS, greet_column, 0)

    order = [(2, 1), (1, 1), (3, 1), (0, 1), (2, 0), (1, 0), (3, 0), (0, 0)]
    loads, swaps = {}, {}
    for dy, dx in order:
        k = dy * 2 + dx
        loads[dy, dx] = pltpu.make_async_copy(
            grads.at[index_of(y + dy, x + dx, core)], own.at[k], local_sem.at[k]
        )
        loads[dy, dx].start()
    pl.semaphore_wait(barrier, REPLICAS - 1 + COLUMNS - 1)
    for dy, dx in order:
        k = dy * 2 + dx
        swaps[dy, dx] = remote(
            grads.at[index_of(y + dy, x + dx, core + 1)],
            twin.at[k],
            core_send.at[k],
            core_recv.at[k],
            dp=index_of(y, x, core + 1),
        )
        swaps[dy, dx].start()

    x_first, y_first, y_second = {}, {}, {}
    used = 0
    for dy, dx in order:
        k = dy * 2 + dx
        loads[dy, dx].wait()
        swaps[dy, dx].wait_recv()
        own[k] = own[k] + twin[k]
        if dx == 1:
            x_first[dy] = remote(
                own.at[k, XS], x_in.at[dy], send.at[used], recv.at[used], dp=index_of(y, x + 1, core)
            )
            x_first[dy].start()
            used += 1
        if dy:
            y_first[dy, dx] = remote(
                own.at[k, YS],
                y_in.at[dy - 1, dx],
                send.at[used],
                recv.at[used],
                dp=index_of(y + dy, x, core),
            )
            y_first[dy, dx].start()
            used += 1
    for dy in (2, 1, 3):
        x_first[dy].wait_recv()
        own[dy * 2, XS] = own[dy * 2, XS] + x_in[dy]
        y_second[dy] = remote(
            own.at[dy * 2, XS],
            y_late.at[dy - 1],
            send.at[used],
            recv.at[used],
            dp=index_of(y + dy, x, core),
        )
        y_second[dy].start()
        used += 1
    for dy in (2, 1, 3):
        y_first[dy, 1].wait_recv()
    own[1, YS] = (
        (own[1, YS].astype(F32) + y_in[0, 1].astype(F32))
        + (y_in[1, 1].astype(F32) + y_in[2, 1].astype(F32))
    ).astype(BF)
    x_second = remote(
        own.at[1, YS], x_late, send.at[used], recv.at[used], dp=index_of(y, x + 1, core)
    )
    x_second.start()
    for dy in (2, 1, 3):
        y_first[dy, 0].wait_recv()
    x_first[0].wait_recv()
    for dy in (2, 1, 3):
        y_second[dy].wait_recv()
    mean_x = (
        (own[0, XS].astype(F32) + x_in[0].astype(F32))
        + (y_late[0].astype(F32) + y_late[1].astype(F32))
        + y_late[2].astype(F32)
    ) * (1.0 / REPLICAS)
    low_out[XS] = mean_x.astype(BF)
    x_second.wait_recv()
    mean_y = (
        (own[0, YS].astype(F32) + x_late[...].astype(F32))
        + (y_in[0, 0].astype(F32) + y_in[1, 0].astype(F32))
        + y_in[2, 0].astype(F32)
    ) * (1.0 / REPLICAS)
    low_out[YS] = mean_y.astype(BF)
    squares = jnp.sum((mean_x * mean_x).reshape(X_ROWS // 8, 8, SIDE), axis=0) + jnp.sum(
        (mean_y * mean_y).reshape(Y_ROWS // 8, 8, SIDE), axis=0
    )
    tile[0] = (squares[:, :128] + squares[:, 128:256]) + (squares[:, 256:384] + squares[:, 384:])

    def ring_copy(step):
        return remote(
            tile.at[0],
            tile.at[step],
            ring_send.at[step],
            ring_recv.at[step],
            dp=(me + step) % REPLICAS,
        )

    def column_copy(step):
        return remote(
            tile2.at[0],
            tile2.at[step],
            column_send.at[step],
            column_recv.at[step],
            fsdp=(column + step) % COLUMNS,
        )

    lax.fori_loop(1, REPLICAS, lambda step, carry: (ring_copy(step).start(), carry)[1], 0)
    lax.fori_loop(1, REPLICAS, lambda step, carry: (ring_copy(step).wait_recv(), carry)[1], 0)
    tile2[0] = jnp.sum(tile[...], axis=0)
    lax.fori_loop(1, COLUMNS, lambda step, carry: (column_copy(step).start(), carry)[1], 0)
    lax.fori_loop(1, COLUMNS, lambda step, carry: (column_copy(step).wait_recv(), carry)[1], 0)
    total_out[...] = jnp.sum(tile2[...], axis=0)

    lax.fori_loop(1, REPLICAS, lambda step, carry: (ring_copy(step).wait_send(), carry)[1], 0)
    lax.fori_loop(1, COLUMNS, lambda step, carry: (column_copy(step).wait_send(), carry)[1], 0)
    for group in (swaps, x_first, y_first, y_second):
        for copy in group.values():
            copy.wait_send()
    x_second.wait_send()


def reduce_grads(grads):
    vmem = pl.BlockSpec(memory_space=pltpu.VMEM)
    dma = pltpu.SemaphoreType.DMA
    return pl.pallas_call(
        reduce_kernel,
        out_shape=(
            jax.ShapeDtypeStruct((SIDE, SIDE), BF),
            jax.ShapeDtypeStruct((8, 128), F32),
        ),
        in_specs=[pl.BlockSpec(memory_space=pl.ANY)],
        out_specs=(vmem, vmem),
        scratch_shapes=[
            pltpu.VMEM((8, SIDE, SIDE), BF),
            pltpu.VMEM((8, SIDE, SIDE), BF),
            pltpu.VMEM((4, X_ROWS, SIDE), BF),
            pltpu.VMEM((3, 2, Y_ROWS, SIDE), BF),
            pltpu.VMEM((3, X_ROWS, SIDE), BF),
            pltpu.VMEM((Y_ROWS, SIDE), BF),
            pltpu.VMEM((REPLICAS, 8, 128), F32),
            pltpu.VMEM((COLUMNS, 8, 128), F32),
            dma((8,)),
            dma((8,)),
            dma((8,)),
            dma((14,)),
            dma((14,)),
            dma((REPLICAS,)),
            dma((REPLICAS,)),
            dma((COLUMNS,)),
            dma((COLUMNS,)),
        ],
        compiler_params=pltpu.CompilerParams(
            collective_id=0, has_side_effects=True, vmem_limit_bytes=40 * 2**20
        ),
        cost_estimate=pl.CostEstimate(flops=0, bytes_accessed=16 * 2**20, transcendentals=0),
        name="reduce_grads",
    )(grads)


def spread_kernel(
    param,
    state,
    rotation,
    params_out,
    state_out,
    gathered,
    rolled,
    local_sem,
    send,
    recv,
    core_send,
    core_recv,
    first_send,
    first_recv,
    second_send,
    second_recv,
):
    me, y, x, core = place()
    barrier = pltpu.get_barrier_semaphore()
    greet_replicas(barrier, me)
    keep = pltpu.make_async_copy(param, params_out.at[me], local_sem.at[0])
    keep.start()
    pl.semaphore_wait(barrier, REPLICAS - 1)

    beside = index_of(y, x + 1, core)
    twin = index_of(y, x, core + 1)
    used = [0]
    used_core = [0]

    def pass_on(src, owner, rows, target):
        copy = remote(
            src, params_out.at[owner, rows], send.at[used[0]], recv.at[used[0]], dp=target
        )
        used[0] += 1
        copy.start()
        return copy

    twins = []

    def to_twin(src, owner, rows):
        k = used_core[0]
        used_core[0] += 1
        copy = remote(src, params_out.at[owner, rows], core_send.at[k], core_recv.at[k], dp=twin)
        copy.start()
        twins.append(copy)

    copies = []
    x_own = pass_on(param.at[YS], me, YS, beside)
    y_own = {dy: pass_on(param.at[XS], me, XS, index_of(y + dy, x, core)) for dy in (2, 1, 3)}
    x_same = pass_on(param.at[XS], me, XS, beside)
    y_same = {dy: pass_on(param.at[YS], me, YS, index_of(y + dy, x, core)) for dy in (2, 1, 3)}
    to_twin(param, me, pl.ds(0, SIDE))

    def first_copy(step):
        return remote(
            state.at[(me + step) % REPLICAS],
            gathered.at[me],
            first_send.at[step],
            first_recv.at[step],
            dp=(me + step) % REPLICAS,
        )

    def second_copy(step):
        return remote(
            rolled.at[(me + step) % REPLICAS],
            state_out.at[me],
            second_send.at[step],
            second_recv.at[step],
            dp=(me + step) % REPLICAS,
        )

    lax.fori_loop(1, REPLICAS, lambda step, carry: (first_copy(step).start(), carry)[1], 0)
    mine = pltpu.make_async_copy(state.at[me], gathered.at[me], local_sem.at[1])
    mine.start()

    x_own.wait_recv()
    y_pair = {
        dy: pass_on(params_out.at[beside, YS], beside, YS, index_of(y + dy, x, core))
        for dy in (2, 1, 3)
    }
    to_twin(params_out.at[beside, YS], beside, YS)
    x_pass = {}
    for dy in (2, 1, 3):
        y_own[dy].wait_recv()
        owner = index_of(y - dy, x, core)
        x_pass[dy] = pass_on(params_out.at[owner, XS], owner, XS, beside)
        to_twin(params_out.at[owner, XS], owner, XS)
    x_same.wait_recv()
    to_twin(params_out.at[beside, XS], beside, XS)
    for dy in (2, 1, 3):
        y_same[dy].wait_recv()
        owner = index_of(y - dy, x, core)
        to_twin(params_out.at[owner, YS], owner, YS)
    for dy in (2, 1, 3):
        y_pair[dy].wait_recv()
        owner = index_of(y - dy, x + 1, core)
        to_twin(params_out.at[owner, YS], owner, YS)
    for dy in (2, 1, 3):
        x_pass[dy].wait_recv()
        owner = index_of(y - dy, x + 1, core)
        to_twin(params_out.at[owner, XS], owner, XS)

    lax.fori_loop(1, REPLICAS, lambda step, carry: (first_copy(step).wait_recv(), carry)[1], 0)
    mine.wait()
    shift = rotation[0]

    def roll(step, carry):
        rolled[step] = gathered[(step + REPLICAS - shift) % REPLICAS]
        return carry

    lax.fori_loop(0, REPLICAS, roll, 0)
    lax.fori_loop(1, REPLICAS, lambda step, carry: (second_copy(step).start(), carry)[1], 0)
    back = pltpu.make_async_copy(rolled.at[me], state_out.at[me], local_sem.at[2])
    back.start()
    keep.wait()
    for copy in twins:
        copy.wait()
    for group in (y_own, y_same, y_pair, x_pass):
        for copy in group.values():
            copy.wait_send()
    x_own.wait_send()
    x_same.wait_send()
    lax.fori_loop(1, REPLICAS, lambda step, carry: (first_copy(step).wait_send(), carry)[1], 0)
    lax.fori_loop(1, REPLICAS, lambda step, carry: (second_copy(step).wait(), carry)[1], 0)
    back.wait()


def spread(param, state, rotation):
    hbm = pl.BlockSpec(memory_space=pl.ANY)
    dma = pltpu.SemaphoreType.DMA
    rows = state.shape[1]
    return pl.pallas_call(
        spread_kernel,
        out_shape=(
            jax.ShapeDtypeStruct((REPLICAS, SIDE, SIDE), BF),
            jax.ShapeDtypeStruct(state.shape, BF),
        ),
        in_specs=[hbm, hbm, pl.BlockSpec(memory_space=pltpu.SMEM)],
        out_specs=(hbm, hbm),
        scratch_shapes=[
            pltpu.VMEM((REPLICAS, rows, SIDE), BF),
            pltpu.VMEM((REPLICAS, rows, SIDE), BF),
            dma((3,)),
            dma((14,)),
            dma((14,)),
            dma((15,)),
            dma((15,)),
            dma((REPLICAS,)),
            dma((REPLICAS,)),
            dma((REPLICAS,)),
            dma((REPLICAS,)),
        ],
        compiler_params=pltpu.CompilerParams(
            collective_id=1, has_side_effects=True, vmem_limit_bytes=40 * 2**20
        ),
        cost_estimate=pl.CostEstimate(flops=0, bytes_accessed=32 * 2**20, transcendentals=0),
        name="spread",
    )(param, state, rotation)


def dot(a, b):
    return jnp.dot(a, b, preferred_element_type=F32)


def orthonormal(factor, basis_start):
    factor_low = factor.astype(BF)
    basis_now = basis_start
    for repeat in range(ITERS):
        image = dot(factor_low, basis_now)
        magnitude = jnp.abs(image)
        bound = (
            jnp.sqrt(jnp.max(jnp.sum(magnitude, axis=0)) * jnp.max(jnp.sum(magnitude, axis=1)))
            + 1e-06
        )
        iterate = image * (1.0 / bound)
        for newton_step in range(NEWTON):
            low = iterate.astype(BF)
            gram = dot(low.T, low).astype(BF)
            iterate = 1.5 * iterate - 0.5 * dot(low, gram)
        basis_now = iterate.astype(BF)
    return basis_now


def local(
    grads,
    left_factor,
    right_factor,
    left_basis,
    right_basis,
    first_moment,
    second_moment,
    parameters,
    rotation,
):
    grad_low, squares = reduce_grads(grads[0, :, 0])
    square_sum = jnp.sum(squares)
    entries = SIDE * SIDE * REPLICAS * COLUMNS
    clip_factor = jnp.minimum(1.0, CLIP_RMS * math.sqrt(entries) / jnp.sqrt(square_sum + 1e-06))
    left_old, right_old = left_basis[0, 0], right_basis[0, 0]
    half_left = dot(left_old.T, grad_low).astype(BF)
    rotated = clip_factor * dot(half_left, right_old)
    moment = BETA_MOMENT * first_moment[0, 0].astype(F32) + (1.0 - BETA_MOMENT) * rotated
    second_new = BETA_SECOND * second_moment[0, 0] + (1.0 - BETA_SECOND) * rotated * rotated
    direction = (moment / (jnp.sqrt(second_new) + TINY)).astype(BF)
    half_back = dot(left_old, direction).astype(BF)
    update = dot(half_back, right_old.T)
    param_new = (parameters[0, 0].astype(F32) - STEP_RATE * update).astype(BF)
    weight = (1.0 - BETA_FACTOR) * (clip_factor * clip_factor)
    left_new = BETA_FACTOR * left_factor[0, 0] + weight * dot(grad_low, grad_low.T)
    right_new = BETA_FACTOR * right_factor[0, 0] + weight * dot(grad_low.T, grad_low)
    left_turned = orthonormal(left_new, left_old)
    right_turned = orthonormal(right_new, right_old)
    left_turn = dot(left_turned.T, left_old).astype(BF)
    right_turn = dot(right_old.T, right_turned).astype(BF)
    first_new = dot(dot(left_turn, moment.astype(BF)).astype(BF), right_turn).astype(BF)
    state = jnp.concatenate(
        [
            value.astype(BF).reshape(REPLICAS, CHUNK, SIDE)
            for value in (left_new, right_new, second_new, left_turned, right_turned, first_new)
        ],
        axis=1,
    )
    gathered, moved = spread(param_new, state, rotation)
    outs = [
        moved[:, CHUNK * k : CHUNK * (k + 1)].reshape(1, 1, SIDE, SIDE) for k in range(6)
    ]
    return (
        gathered[:, None],
        outs[0].astype(F32),
        outs[1].astype(F32),
        outs[3],
        outs[4],
        outs[5],
        outs[2].astype(F32),
    )


def solution(mesh):
    state = P("dp", "fsdp", None, None)
    return jax.shard_map(
        local,
        mesh=mesh,
        in_specs=(P("dp", None, "fsdp", None, None),) + (state,) * 7 + (P("fsdp"),),
        out_specs=(P(None, "fsdp", None, None),) + (state,) * 6,
        check_vma=False,
    )
```

```python
import math

import jax
import jax.numpy as jnp
from jax import lax
from jax.experimental import pallas as pl
from jax.experimental.pallas import tpu as pltpu
from jax.sharding import PartitionSpec as P

ITERS = 2
NEWTON = 3
SIDE = 512
REPLICAS = 16
COLUMNS = 8
CHUNK = SIDE // REPLICAS

BETA_MOMENT = 0.95
BETA_SECOND = 0.95
BETA_FACTOR = 0.95
STEP_RATE = 0.05
CLIP_RMS = 0.3
TINY = 1e-08

Y_ROWS = 208
X_ROWS = SIDE - Y_ROWS
YS = pl.ds(0, Y_ROWS)
XS = pl.ds(Y_ROWS, X_ROWS)

MESH = pl.DeviceIdType.MESH
BF = jnp.bfloat16
F32 = jnp.float32


def place():
    me = lax.axis_index("dp")
    return me, me // 4, me // 2 % 2, me % 2


def index_of(y, x, core):
    return y % 4 * 4 + x % 2 * 2 + core % 2


def remote(src, dst, send, recv, **where):
    return pltpu.make_async_remote_copy(
        src_ref=src, dst_ref=dst, send_sem=send, recv_sem=recv, device_id=where, device_id_type=MESH
    )


def greet_replicas(barrier, me):
    def greet(step, carry):
        pl.semaphore_signal(
            barrier, inc=1, device_id={"dp": (me + step) % REPLICAS}, device_id_type=MESH
        )
        return carry

    lax.fori_loop(1, REPLICAS, greet, 0)


def nn(a, b):
    return jnp.dot(a, b, preferred_element_type=F32)


def nt(a, b):
    return lax.dot_general(a, b, (((1,), (1,)), ((), ())), preferred_element_type=F32)


def tn(a, b):
    return lax.dot_general(a, b, (((0,), (0,)), ((), ())), preferred_element_type=F32)


def each(count, act):
    lax.fori_loop(1, count, lambda step, carry: (act(step), carry)[1], 0)


def chunked(value):
    return value.reshape(REPLICAS, CHUNK, SIDE)


def image_step(factor, basis, iterate, low):
    image = nn(factor, basis)
    magnitude = jnp.abs(image)
    bound = (
        jnp.sqrt(jnp.max(jnp.sum(magnitude, axis=0)) * jnp.max(jnp.sum(magnitude, axis=1)))
        + 1e-06
    )
    scaled = image * (1.0 / bound)
    iterate[...] = scaled
    low[...] = scaled.astype(BF)


def newton_step(iterate, low, gram):
    gram[...] = nt(low[...], low[...]).astype(BF)
    value = 1.5 * iterate[...] - 0.5 * nn(gram[...], low[...])
    iterate[...] = value
    low[...] = value.astype(BF)


def step_kernel(
    grads,
    left_hbm,
    right_hbm,
    second_hbm,
    left_basis_hbm,
    right_basis_hbm,
    first_hbm,
    param_hbm,
    rotation,
    params_out,
    wide_out,
    narrow_out,
    own,
    twin,
    x_in,
    y_in,
    y_late,
    x_late,
    tile,
    tile2,
    left_old,
    right_old,
    second_old,
    left_basis,
    right_basis,
    first_old,
    param_old,
    grad_low,
    rotated,
    moment_low,
    left_iter,
    right_iter,
    left_low,
    right_low,
    left_gram,
    right_gram,
    wide,
    narrow,
    wide_in,
    narrow_in,
    wide_rolled,
    narrow_rolled,
    local_sem,
    load_sem,
    core_send,
    core_recv,
    send,
    recv,
    ring_send,
    ring_recv,
    column_send,
    column_recv,
    ag_send,
    ag_recv,
    twin_send,
    twin_recv,
    wide_send,
    wide_recv,
    wide_send2,
    wide_recv2,
    narrow_send,
    narrow_recv,
    narrow_send2,
    narrow_recv2,
):
    me, y, x, core = place()
    column = lax.axis_index("fsdp")
    barrier = pltpu.get_barrier_semaphore()
    greet_replicas(barrier, me)
    def greet_column(step, carry):
        pl.semaphore_signal(
            barrier, inc=1, device_id={"fsdp": (column + step) % COLUMNS}, device_id_type=MESH
        )
        return carry

    lax.fori_loop(1, COLUMNS, greet_column, 0)

    order = [(2, 1), (1, 1), (3, 1), (0, 1), (2, 0), (1, 0), (3, 0), (0, 0)]
    loads, swaps = {}, {}
    for dy, dx in order:
        k = dy * 2 + dx
        loads[dy, dx] = pltpu.make_async_copy(
            grads.at[index_of(y + dy, x + dx, core)], own.at[k], local_sem.at[k]
        )
        loads[dy, dx].start()
    pl.semaphore_wait(barrier, REPLICAS - 1 + COLUMNS - 1)
    for dy, dx in order:
        k = dy * 2 + dx
        swaps[dy, dx] = remote(
            grads.at[index_of(y + dy, x + dx, core + 1)],
            twin.at[k],
            core_send.at[k],
            core_recv.at[k],
            dp=index_of(y, x, core + 1),
        )
        swaps[dy, dx].start()

    state_loads = [
        pltpu.make_async_copy(source, target, load_sem.at[k])
        for k, (source, target) in enumerate(
            (
                (left_basis_hbm, left_basis),
                (right_basis_hbm, right_basis),
                (first_hbm, first_old),
                (second_hbm, second_old),
                (left_hbm, left_old),
                (right_hbm, right_old),
                (param_hbm, param_old),
            )
        )
    ]
    for load in state_loads:
        load.start()

    x_first, y_first, y_second = {}, {}, {}
    used = 0
    for dy, dx in order:
        k = dy * 2 + dx
        loads[dy, dx].wait()
        swaps[dy, dx].wait_recv()
        own[k] = own[k] + twin[k]
        if dx == 1:
            x_first[dy] = remote(
                own.at[k, XS], x_in.at[dy], send.at[used], recv.at[used], dp=index_of(y, x + 1, core)
            )
            x_first[dy].start()
            used += 1
        if dy:
            y_first[dy, dx] = remote(
                own.at[k, YS],
                y_in.at[dy - 1, dx],
                send.at[used],
                recv.at[used],
                dp=index_of(y + dy, x, core),
            )
            y_first[dy, dx].start()
            used += 1
    for dy in (2, 1, 3):
        x_first[dy].wait_recv()
        own[dy * 2, XS] = own[dy * 2, XS] + x_in[dy]
        y_second[dy] = remote(
            own.at[dy * 2, XS],
            y_late.at[dy - 1],
            send.at[used],
            recv.at[used],
            dp=index_of(y + dy, x, core),
        )
        y_second[dy].start()
        used += 1
    for dy in (2, 1, 3):
        y_first[dy, 1].wait_recv()
    own[1, YS] = (
        (own[1, YS].astype(F32) + y_in[0, 1].astype(F32))
        + (y_in[1, 1].astype(F32) + y_in[2, 1].astype(F32))
    ).astype(BF)
    x_second = remote(
        own.at[1, YS], x_late, send.at[used], recv.at[used], dp=index_of(y, x + 1, core)
    )
    x_second.start()
    for dy in (2, 1, 3):
        y_first[dy, 0].wait_recv()
    x_first[0].wait_recv()
    for dy in (2, 1, 3):
        y_second[dy].wait_recv()
    mean_x = (
        (own[0, XS].astype(F32) + x_in[0].astype(F32))
        + (y_late[0].astype(F32) + y_late[1].astype(F32))
        + y_late[2].astype(F32)
    ) * (1.0 / REPLICAS)
    grad_low[XS] = mean_x.astype(BF)
    x_second.wait_recv()
    mean_y = (
        (own[0, YS].astype(F32) + x_late[...].astype(F32))
        + (y_in[0, 0].astype(F32) + y_in[1, 0].astype(F32))
        + y_in[2, 0].astype(F32)
    ) * (1.0 / REPLICAS)
    grad_low[YS] = mean_y.astype(BF)
    squares = jnp.sum((mean_x * mean_x).reshape(X_ROWS // 8, 8, SIDE), axis=0) + jnp.sum(
        (mean_y * mean_y).reshape(Y_ROWS // 8, 8, SIDE), axis=0
    )
    tile[0] = (squares[:, :128] + squares[:, 128:256]) + (squares[:, 256:384] + squares[:, 384:])

    def ring_copy(step):
        return remote(
            tile.at[0],
            tile.at[step],
            ring_send.at[step],
            ring_recv.at[step],
            dp=(me + step) % REPLICAS,
        )

    def column_copy(step):
        return remote(
            tile2.at[0],
            tile2.at[step],
            column_send.at[step],
            column_recv.at[step],
            fsdp=(column + step) % COLUMNS,
        )

    each(REPLICAS, lambda step: ring_copy(step).start())
    for load in state_loads:
        load.wait()
    half_left = tn(left_basis[...], grad_low[...]).astype(BF)
    rotated[...] = nn(half_left, right_basis[...])
    each(REPLICAS, lambda step: ring_copy(step).wait_recv())
    tile2[0] = jnp.sum(tile[...], axis=0)
    each(COLUMNS, lambda step: column_copy(step).start())
    left_iter[...] = nt(grad_low[...], grad_low[...])
    right_iter[...] = tn(grad_low[...], grad_low[...])
    each(COLUMNS, lambda step: column_copy(step).wait_recv())
    square_sum = jnp.sum(jnp.sum(tile2[...], axis=0))
    entries = SIDE * SIDE * REPLICAS * COLUMNS
    clip_factor = jnp.minimum(1.0, CLIP_RMS * math.sqrt(entries) / jnp.sqrt(square_sum + 1e-06))

    def state_copy(source, target, sends, recvs, step):
        there = (me + step) % REPLICAS
        return remote(
            source.at[there], target.at[me], sends.at[step], recvs.at[step], dp=there
        )

    def wide_copy(step):
        return state_copy(wide, wide_in, wide_send, wide_recv, step)

    def narrow_copy(step):
        return state_copy(narrow, narrow_in, narrow_send, narrow_recv, step)

    def wide_copy2(step):
        return state_copy(wide_rolled, wide_out, wide_send2, wide_recv2, step)

    def narrow_copy2(step):
        return state_copy(narrow_rolled, narrow_out, narrow_send2, narrow_recv2, step)

    weight = (1.0 - BETA_FACTOR) * (clip_factor * clip_factor)
    left_new = (BETA_FACTOR * left_old[...] + weight * left_iter[...]).astype(BF)
    right_new = (BETA_FACTOR * right_old[...] + weight * right_iter[...]).astype(BF)
    wide[:, 0:CHUNK] = chunked(left_new)
    wide[:, CHUNK : 2 * CHUNK] = chunked(right_new)
    turned = clip_factor * rotated[...]
    moment = BETA_MOMENT * first_old[...].astype(F32) + (1.0 - BETA_MOMENT) * turned
    second_new = BETA_SECOND * second_old[...] + (1.0 - BETA_SECOND) * turned * turned
    wide[:, 2 * CHUNK : 3 * CHUNK] = chunked(second_new.astype(BF))
    moment_low[...] = moment.astype(BF)
    direction = (moment / (jnp.sqrt(second_new) + TINY)).astype(BF)
    each(REPLICAS, lambda step: wide_copy(step).start())
    wide_in[me] = wide[me]

    half_back = nn(left_basis[...], direction).astype(BF)
    update = nt(half_back, right_basis[...])
    params_out[me] = (param_old[...].astype(F32) - STEP_RATE * update).astype(BF)

    beside = index_of(y, x + 1, core)
    other = index_of(y, x, core + 1)
    counts = [0, 0]
    copies = []

    def pass_on(owner, rows, target):
        k = counts[0]
        counts[0] += 1
        view = params_out.at[owner, rows]
        copy = remote(view, view, ag_send.at[k], ag_recv.at[k], dp=target)
        copy.start()
        copies.append(copy)
        return copy

    twins = []

    def to_twin(owner, rows):
        k = counts[1]
        counts[1] += 1
        view = params_out.at[owner, rows]
        copy = remote(view, view, twin_send.at[k], twin_recv.at[k], dp=other)
        copy.start()
        twins.append(copy)

    x_own = pass_on(me, YS, beside)
    y_own = {dy: pass_on(me, XS, index_of(y + dy, x, core)) for dy in (2, 1, 3)}
    x_same = pass_on(me, XS, beside)
    y_same = {dy: pass_on(me, YS, index_of(y + dy, x, core)) for dy in (2, 1, 3)}
    to_twin(me, pl.ds(0, SIDE))

    for repeat in range(ITERS):
        left_start = left_basis if repeat == 0 else left_low
        right_start = right_basis if repeat == 0 else right_low
        image_step(
            wide[:, 0:CHUNK].reshape(SIDE, SIDE), left_start[...], left_iter, left_low
        )
        image_step(
            wide[:, CHUNK : 2 * CHUNK].reshape(SIDE, SIDE), right_start[...], right_iter, right_low
        )
        for newton in range(NEWTON):
            newton_step(left_iter, left_low, left_gram)
            newton_step(right_iter, right_low, right_gram)
    narrow[:, 0:CHUNK] = chunked(left_low[...])
    narrow[:, CHUNK : 2 * CHUNK] = chunked(right_low[...])
    left_turn = tn(left_low[...], left_basis[...]).astype(BF)
    right_turn = tn(right_basis[...], right_low[...]).astype(BF)
    half_turned = nn(left_turn, moment_low[...]).astype(BF)
    narrow[:, 2 * CHUNK : 3 * CHUNK] = chunked(nn(half_turned, right_turn).astype(BF))
    each(REPLICAS, lambda step: narrow_copy(step).start())
    narrow_in[me] = narrow[me]

    shift = rotation[0]

    def roll(source, rolled, target, copy):
        def one(step):
            there = (me + step) % REPLICAS
            rolled[there] = source[(there + REPLICAS - shift) % REPLICAS]
            copy(step).start()

        each(REPLICAS, one)
        target[me] = source[(me + REPLICAS - shift) % REPLICAS]

    x_own.wait_recv()
    y_pair = {dy: pass_on(beside, YS, index_of(y + dy, x, core)) for dy in (2, 1, 3)}
    to_twin(beside, YS)
    x_pass = {}
    for dy in (2, 1, 3):
        y_own[dy].wait_recv()
        owner = index_of(y - dy, x, core)
        x_pass[dy] = pass_on(owner, XS, beside)
        to_twin(owner, XS)
    each(REPLICAS, lambda step: wide_copy(step).wait_recv())
    roll(wide_in, wide_rolled, wide_out, wide_copy2)
    x_same.wait_recv()
    to_twin(beside, XS)
    for dy in (2, 1, 3):
        y_same[dy].wait_recv()
        to_twin(index_of(y - dy, x, core), YS)
    each(REPLICAS, lambda step: narrow_copy(step).wait_recv())
    roll(narrow_in, narrow_rolled, narrow_out, narrow_copy2)
    for dy in (2, 1, 3):
        y_pair[dy].wait_recv()
        to_twin(index_of(y - dy, x + 1, core), YS)
    for dy in (2, 1, 3):
        x_pass[dy].wait_recv()
        to_twin(index_of(y - dy, x + 1, core), XS)

    for group in (swaps, x_first, y_first, y_second):
        for copy in group.values():
            copy.wait_send()
    x_second.wait_send()
    each(REPLICAS, lambda step: ring_copy(step).wait_send())
    each(COLUMNS, lambda step: column_copy(step).wait_send())
    for copy in twins:
        copy.wait()
    for copy in copies:
        copy.wait_send()
    each(REPLICAS, lambda step: wide_copy(step).wait_send())
    each(REPLICAS, lambda step: narrow_copy(step).wait_send())
    each(REPLICAS, lambda step: wide_copy2(step).wait())
    each(REPLICAS, lambda step: narrow_copy2(step).wait())


def step(arrays, rotation):
    hbm = pl.BlockSpec(memory_space=pl.ANY)
    dma = pltpu.SemaphoreType.DMA
    moved = (REPLICAS, 3 * CHUNK, SIDE)

    def block(dtype):
        return pltpu.VMEM((SIDE, SIDE), dtype)

    arrays = [pltpu.with_memory_space_constraint(array, pltpu.HBM) for array in arrays]
    return pl.pallas_call(
        step_kernel,
        out_shape=(
            pltpu.VMEM((REPLICAS, SIDE, SIDE), BF),
            pltpu.VMEM(moved, BF),
            pltpu.VMEM(moved, BF),
        ),
        in_specs=[hbm] * len(arrays) + [pl.BlockSpec(memory_space=pltpu.SMEM)],
        out_specs=(pl.BlockSpec(memory_space=pltpu.VMEM),) * 3,
        scratch_shapes=[
            pltpu.VMEM((8, SIDE, SIDE), BF),
            pltpu.VMEM((8, SIDE, SIDE), BF),
            pltpu.VMEM((4, X_ROWS, SIDE), BF),
            pltpu.VMEM((3, 2, Y_ROWS, SIDE), BF),
            pltpu.VMEM((3, X_ROWS, SIDE), BF),
            pltpu.VMEM((Y_ROWS, SIDE), BF),
            pltpu.VMEM((REPLICAS, 8, 128), F32),
            pltpu.VMEM((COLUMNS, 8, 128), F32),
            block(F32),
            block(F32),
            block(F32),
            block(BF),
            block(BF),
            block(BF),
            block(BF),
            block(BF),
            block(F32),
            block(BF),
            block(F32),
            block(F32),
            block(BF),
            block(BF),
            block(BF),
            block(BF),
        ]
        + [pltpu.VMEM(moved, BF)] * 6
        + [dma((8,)), dma((7,)), dma((8,)), dma((8,)), dma((14,)), dma((14,))]
        + [dma((REPLICAS,))] * 2
        + [dma((COLUMNS,))] * 2
        + [dma((14,))] * 2
        + [dma((15,))] * 2
        + [dma((REPLICAS,))] * 8,
        compiler_params=pltpu.CompilerParams(
            collective_id=0, has_side_effects=True, vmem_limit_bytes=46 * 2**20
        ),
        cost_estimate=pl.CostEstimate(
            flops=10**10, bytes_accessed=32 * 2**20, transcendentals=0
        ),
        name="soap_step",
    )(*arrays, rotation)


def finish_kernel(params, wide, narrow, params_out, left, right, second, *rest):
    left_basis, right_basis, first, staged, sems = rest
    copies = [pltpu.make_async_copy(params, params_out, sems.at[0])]
    for k, target in enumerate((left_basis, right_basis, first)):
        copies.append(
            pltpu.make_async_copy(
                narrow.at[:, pl.ds(CHUNK * k, CHUNK)], target, sems.at[1 + k]
            )
        )
    for copy in copies:
        copy.start()
    for k, target in enumerate((left, right, second)):
        staged[k] = wide[:, CHUNK * k : CHUNK * (k + 1)].astype(F32)
        copies.append(pltpu.make_async_copy(staged.at[k], target, sems.at[4 + k]))
        copies[-1].start()
    for copy in copies:
        copy.wait()


def finish(params, wide, narrow):
    hbm = pl.BlockSpec(memory_space=pl.ANY)
    vmem = pl.BlockSpec(memory_space=pltpu.VMEM)
    slots = (REPLICAS, CHUNK, SIDE)
    return pl.pallas_call(
        finish_kernel,
        out_shape=(pltpu.HBM((REPLICAS, SIDE, SIDE), BF),)
        + (pltpu.HBM(slots, F32),) * 3
        + (pltpu.HBM(slots, BF),) * 3,
        in_specs=[vmem, vmem, vmem],
        out_specs=(hbm,) * 7,
        scratch_shapes=[
            pltpu.VMEM((3,) + slots, F32),
            pltpu.SemaphoreType.DMA((7,)),
        ],
        compiler_params=pltpu.CompilerParams(vmem_limit_bytes=24 * 2**20),
        cost_estimate=pl.CostEstimate(flops=0, bytes_accessed=24 * 2**20, transcendentals=0),
        name="finish",
    )(params, wide, narrow)


def local(
    grads,
    left_factor,
    right_factor,
    left_basis,
    right_basis,
    first_moment,
    second_moment,
    parameters,
    rotation,
):
    blocks = (
        left_factor,
        right_factor,
        second_moment,
        left_basis,
        right_basis,
        first_moment,
        parameters,
    )
    params, wide, narrow = step([grads[0, :, 0]] + [value[0, 0] for value in blocks], rotation)
    gathered, *outs = finish(params, wide, narrow)
    left, right, second, left_turned, right_turned, first = (
        value.reshape(1, 1, SIDE, SIDE) for value in outs
    )
    return (gathered[:, None], left, right, left_turned, right_turned, first, second)


def solution(mesh):
    state = P("dp", "fsdp", None, None)
    return jax.shard_map(
        local,
        mesh=mesh,
        in_specs=(P("dp", None, "fsdp", None, None),) + (state,) * 7 + (P("fsdp"),),
        out_specs=(P(None, "fsdp", None, None),) + (state,) * 6,
        check_vma=False,
    )
```

```python
import math

import jax
import jax.numpy as jnp
from jax import lax
from jax.experimental import pallas as pl
from jax.experimental.pallas import tpu as pltpu
from jax.sharding import PartitionSpec as P

ITERS = 2
NEWTON = 3
SIDE = 512
REPLICAS = 16
COLUMNS = 8
CHUNK = SIDE // REPLICAS

BETA_MOMENT = 0.95
BETA_SECOND = 0.95
BETA_FACTOR = 0.95
STEP_RATE = 0.05
CLIP_RMS = 0.3
TINY = 1e-08

A_HALF = 144
A_ROWS = 2 * A_HALF
B_ROWS = SIDE - A_ROWS
B_HALF = B_ROWS // 2
A = pl.ds(0, A_ROWS)
B = pl.ds(A_ROWS, B_ROWS)
A0, A1 = pl.ds(0, A_HALF), pl.ds(A_HALF, A_HALF)
B0, B1 = pl.ds(A_ROWS, B_HALF), pl.ds(A_ROWS + B_HALF, B_HALF)
LATE0, LATE1 = pl.ds(0, B_HALF), pl.ds(B_HALF, B_HALF)

MESH = pl.DeviceIdType.MESH
BF = jnp.bfloat16
F32 = jnp.float32


def place():
    me = lax.axis_index("dp")
    return me, me // 4, me // 2 % 2, me % 2


def index_of(y, x, core):
    return y % 4 * 4 + x % 2 * 2 + core % 2


def remote(src, dst, send, recv, **where):
    return pltpu.make_async_remote_copy(
        src_ref=src, dst_ref=dst, send_sem=send, recv_sem=recv, device_id=where, device_id_type=MESH
    )


def greet_replicas(barrier, me):
    def greet(step, carry):
        pl.semaphore_signal(
            barrier, inc=1, device_id={"dp": (me + step) % REPLICAS}, device_id_type=MESH
        )
        return carry

    lax.fori_loop(1, REPLICAS, greet, 0)


def nn(a, b):
    return jnp.dot(a, b, preferred_element_type=F32)


def nt(a, b):
    return lax.dot_general(a, b, (((1,), (1,)), ((), ())), preferred_element_type=F32)


def tn(a, b):
    return lax.dot_general(a, b, (((0,), (0,)), ((), ())), preferred_element_type=F32)


def each(count, act):
    lax.fori_loop(1, count, lambda step, carry: (act(step), carry)[1], 0)


def chunked(value):
    return value.reshape(REPLICAS, CHUNK, SIDE)


def image_step(factor, basis, iterate, low):
    image = nn(factor, basis)
    magnitude = jnp.abs(image)
    bound = (
        jnp.sqrt(jnp.max(jnp.sum(magnitude, axis=0)) * jnp.max(jnp.sum(magnitude, axis=1)))
        + 1e-06
    )
    scaled = image * (1.0 / bound)
    iterate[...] = scaled
    low[...] = scaled.astype(BF)


def newton_step(iterate, low, gram):
    gram[...] = nt(low[...], low[...]).astype(BF)
    value = 1.5 * iterate[...] - 0.5 * nn(gram[...], low[...])
    iterate[...] = value
    low[...] = value.astype(BF)


def step_kernel(
    grads,
    left_hbm,
    right_hbm,
    second_hbm,
    left_basis_hbm,
    right_basis_hbm,
    first_hbm,
    param_hbm,
    rotation,
    params_out,
    wide_out,
    narrow_out,
    own,
    twin,
    x_in,
    y_relay,
    y_in,
    late_relay,
    y_late,
    x_late,
    tile,
    tile2,
    left_old,
    right_old,
    second_old,
    left_basis,
    right_basis,
    first_old,
    param_old,
    grad_low,
    rotated,
    moment_low,
    left_iter,
    right_iter,
    left_low,
    right_low,
    left_gram,
    right_gram,
    left_factor,
    old,
    outer,
    old_in,
    outer_in,
    wide,
    wide_in,
    narrow,
    narrow_in,
    wide_rolled,
    narrow_rolled,
    local_sem,
    load_sem,
    core_send,
    core_recv,
    send,
    recv,
    ring_send,
    ring_recv,
    column_send,
    column_recv,
    ag_send,
    ag_recv,
    twin_send,
    twin_recv,
    old_send,
    old_recv,
    old_send2,
    old_recv2,
    outer_send,
    outer_recv,
    wide_send,
    wide_recv,
    wide_send2,
    wide_recv2,
    narrow_send,
    narrow_recv,
    narrow_send2,
    narrow_recv2,
):
    me, y, x, core = place()
    column = lax.axis_index("fsdp")
    barrier = pltpu.get_barrier_semaphore()
    greet_replicas(barrier, me)
    def greet_column(step, carry):
        pl.semaphore_signal(
            barrier, inc=1, device_id={"fsdp": (column + step) % COLUMNS}, device_id_type=MESH
        )
        return carry

    lax.fori_loop(1, COLUMNS, greet_column, 0)

    beside = index_of(y, x + 1, core)
    other = index_of(y, x, core + 1)
    up = index_of(y + 1, x, core)
    down = index_of(y - 1, x, core)
    order = [(2, 1), (2, 0), (1, 1), (3, 1), (1, 0), (3, 0), (0, 1), (0, 0)]
    loads, swaps = {}, {}
    left_load = pltpu.make_async_copy(left_hbm, left_old, load_sem.at[0])
    left_load.start()
    for dy, dx in order:
        k = dy * 2 + dx
        loads[dy, dx] = pltpu.make_async_copy(
            grads.at[index_of(y + dy, x + dx, core)], own.at[k], local_sem.at[k]
        )
        loads[dy, dx].start()
    pl.semaphore_wait(barrier, REPLICAS - 1 + COLUMNS - 1)
    for dy, dx in order:
        k = dy * 2 + dx
        swaps[dy, dx] = remote(
            grads.at[index_of(y + dy, x + dx, core + 1)],
            twin.at[k],
            core_send.at[k],
            core_recv.at[k],
            dp=other,
        )
        swaps[dy, dx].start()

    state_loads = [
        pltpu.make_async_copy(source, target, load_sem.at[1 + k])
        for k, (source, target) in enumerate(
            (
                (left_basis_hbm, left_basis),
                (right_basis_hbm, right_basis),
                (first_hbm, first_old),
                (second_hbm, second_old),
                (right_hbm, right_old),
                (param_hbm, param_old),
            )
        )
    ]
    for load in state_loads:
        load.start()

    def state_copy(source, target, sends, recvs, step, rows=None):
        there = (me + step) % REPLICAS
        if rows is None:
            return remote(
                source.at[there], target.at[me], sends.at[step], recvs.at[step], dp=there
            )
        return remote(
            source.at[there, rows], target.at[me, rows], sends.at[step], recvs.at[step], dp=there
        )

    def old_copy(step):
        return state_copy(old, old_in, old_send, old_recv, step, pl.ds(0, CHUNK // 2))

    def old_copy2(step):
        rows = pl.ds(CHUNK // 2, CHUNK // 2)
        return state_copy(old, old_in, old_send2, old_recv2, step, rows)

    def outer_copy(step):
        return state_copy(outer, outer_in, outer_send, outer_recv, step)

    left_load.wait()
    old[...] = chunked(left_old[...].astype(BF))
    each(REPLICAS, lambda step: old_copy(step).start())
    old_in[me] = old[me]

    links = []

    def link(source, target, device):
        k = len(links)
        copy = remote(source, target, send.at[k], recv.at[k], dp=device)
        copy.start()
        links.append(copy)
        return copy

    def add(k, rows, value):
        own[k, rows] = own[k, rows] + value

    x_first, far_up, far_down, free_up, free_down, near_up, near_down = ({} for _ in range(7))
    for dy, dx in order:
        k = dy * 2 + dx
        loads[dy, dx].wait()
        swaps[dy, dx].wait_recv()
        own[k] = own[k] + twin[k]
        if dx == 1:
            x_first[dy] = link(own.at[k, B], x_in.at[dy], beside)
        if dy == 2:
            far_up[dx] = link(own.at[k, A0], y_relay.at[0, dx], up)
            far_down[dx] = link(own.at[k, A1], y_relay.at[1, dx], down)
        if dy == 1:
            free_up[dx] = link(own.at[k, A1], y_in.at[0, dx, A1], up)
        if dy == 3:
            free_down[dx] = link(own.at[k, A0], y_in.at[1, dx, A0], down)

    def relay_rows(dx):
        far_up[dx].wait_recv()
        add(2 + dx, A0, y_relay[0, dx])
        near_up[dx] = link(own.at[2 + dx, A0], y_in.at[0, dx, A0], up)
        far_down[dx].wait_recv()
        add(6 + dx, A1, y_relay[1, dx])
        near_down[dx] = link(own.at[6 + dx, A1], y_in.at[1, dx, A1], down)

    relay_rows(1)
    x_first[2].wait_recv()
    add(4, B, x_in[2])
    late_far_up = link(own.at[4, B0], late_relay.at[0], up)
    late_far_down = link(own.at[4, B1], late_relay.at[1], down)
    relay_rows(0)
    x_first[1].wait_recv()
    add(2, B, x_in[1])
    late_free_up = link(own.at[2, B1], y_late.at[0, LATE1], up)
    x_first[3].wait_recv()
    add(6, B, x_in[3])
    late_free_down = link(own.at[6, B0], y_late.at[1, LATE0], down)
    for group in (free_up, near_up, free_down, near_down):
        group[1].wait_recv()
    own[1, A] = (
        own[1, A].astype(F32) + (y_in[0, 1].astype(F32) + y_in[1, 1].astype(F32))
    ).astype(BF)
    x_second = link(own.at[1, A], x_late, beside)
    late_far_up.wait_recv()
    add(2, B0, late_relay[0])
    late_near_up = link(own.at[2, B0], y_late.at[0, LATE0], up)
    late_far_down.wait_recv()
    add(6, B1, late_relay[1])
    late_near_down = link(own.at[6, B1], y_late.at[1, LATE1], down)
    each(REPLICAS, lambda step: old_copy2(step).start())
    for group in (free_up, near_up, free_down, near_down):
        group[0].wait_recv()
    x_first[0].wait_recv()
    x_second.wait_recv()
    mean_y = (
        (own[0, A].astype(F32) + x_late[...].astype(F32))
        + (y_in[0, 0].astype(F32) + y_in[1, 0].astype(F32))
    ) * (1.0 / REPLICAS)
    grad_low[A] = mean_y.astype(BF)
    for copy in (late_free_up, late_near_up, late_free_down, late_near_down):
        copy.wait_recv()
    mean_x = (
        (own[0, B].astype(F32) + x_in[0].astype(F32))
        + (y_late[0].astype(F32) + y_late[1].astype(F32))
    ) * (1.0 / REPLICAS)
    grad_low[B] = mean_x.astype(BF)
    squares = jnp.sum((mean_x * mean_x).reshape(B_ROWS // 8, 8, SIDE), axis=0) + jnp.sum(
        (mean_y * mean_y).reshape(A_ROWS // 8, 8, SIDE), axis=0
    )
    tile2[0] = (squares[:, :128] + squares[:, 128:256]) + (squares[:, 256:384] + squares[:, 384:])

    def ring_copy(step):
        return remote(
            tile.at[0],
            tile.at[step],
            ring_send.at[step],
            ring_recv.at[step],
            dp=(me + step) % REPLICAS,
        )

    def column_copy(step):
        return remote(
            tile2.at[0],
            tile2.at[step],
            column_send.at[step],
            column_recv.at[step],
            fsdp=(column + step) % COLUMNS,
        )

    each(COLUMNS, lambda step: column_copy(step).start())
    outer_left = nt(grad_low[...], grad_low[...])
    left_iter[...] = outer_left
    outer[...] = chunked(outer_left.astype(BF))
    outer_in[me] = outer[me]
    for load in state_loads:
        load.wait()
    half_left = tn(left_basis[...], grad_low[...]).astype(BF)
    each(COLUMNS, lambda step: column_copy(step).wait_recv())
    tile[0] = jnp.sum(tile2[...], axis=0)
    each(REPLICAS, lambda step: ring_copy(step).start())
    each(REPLICAS, lambda step: outer_copy(step).start())
    rotated[...] = nn(half_left, right_basis[...])
    right_iter[...] = tn(grad_low[...], grad_low[...])
    each(REPLICAS, lambda step: ring_copy(step).wait_recv())
    square_sum = jnp.sum(jnp.sum(tile[...], axis=0))
    entries = SIDE * SIDE * REPLICAS * COLUMNS
    clip_factor = jnp.minimum(1.0, CLIP_RMS * math.sqrt(entries) / jnp.sqrt(square_sum + 1e-06))

    def wide_copy(step):
        return state_copy(wide, wide_in, wide_send, wide_recv, step)

    def narrow_copy(step):
        return state_copy(narrow, narrow_in, narrow_send, narrow_recv, step)

    def wide_copy2(step):
        return state_copy(wide_rolled, wide_out, wide_send2, wide_recv2, step)

    def narrow_copy2(step):
        return state_copy(narrow_rolled, narrow_out, narrow_send2, narrow_recv2, step)

    weight = (1.0 - BETA_FACTOR) * (clip_factor * clip_factor)
    turned = clip_factor * rotated[...]
    moment = BETA_MOMENT * first_old[...].astype(F32) + (1.0 - BETA_MOMENT) * turned
    second_new = BETA_SECOND * second_old[...] + (1.0 - BETA_SECOND) * turned * turned
    wide[:, CHUNK : 2 * CHUNK] = chunked(second_new.astype(BF))
    moment_low[...] = moment.astype(BF)
    direction = (moment / (jnp.sqrt(second_new) + TINY)).astype(BF)
    half_back = nn(left_basis[...], direction).astype(BF)
    update = nt(half_back, right_basis[...])
    params_out[me] = (param_old[...].astype(F32) - STEP_RATE * update).astype(BF)

    far = index_of(y + 2, x, core)
    beside_down = index_of(y - 1, x + 1, core)
    beside_up = index_of(y + 1, x + 1, core)
    beside_far = index_of(y + 2, x + 1, core)
    copies, twins = [], []

    def pass_on(owner, rows, target):
        k = len(copies)
        view = params_out.at[owner, rows]
        copy = remote(view, view, ag_send.at[k], ag_recv.at[k], dp=target)
        copy.start()
        copies.append(copy)
        return copy

    def to_twin(owner, rows):
        k = len(twins)
        view = params_out.at[owner, rows]
        copy = remote(view, view, twin_send.at[k], twin_recv.at[k], dp=other)
        copy.start()
        twins.append(copy)

    x_own = pass_on(me, A, beside)
    b_up = pass_on(me, B, up)
    b_down = pass_on(me, B, down)
    a_up = pass_on(me, A, up)
    a_down = pass_on(me, A, down)
    x_same = pass_on(me, B, beside)
    to_twin(me, pl.ds(0, SIDE))

    right_new = (BETA_FACTOR * right_old[...] + weight * right_iter[...]).astype(BF)
    wide[:, 0:CHUNK] = chunked(right_new)
    each(REPLICAS, lambda step: wide_copy(step).start())
    wide_in[me] = wide[me]
    left_factor[...] = (BETA_FACTOR * left_old[...] + weight * left_iter[...]).astype(BF)

    for repeat in range(ITERS):
        left_start = left_basis if repeat == 0 else left_low
        right_start = right_basis if repeat == 0 else right_low
        image_step(left_factor[...], left_start[...], left_iter, left_low)
        image_step(
            wide[:, 0:CHUNK].reshape(SIDE, SIDE), right_start[...], right_iter, right_low
        )
        for newton in range(NEWTON):
            newton_step(left_iter, left_low, left_gram)
            newton_step(right_iter, right_low, right_gram)
    narrow[:, 0:CHUNK] = chunked(left_low[...])
    narrow[:, CHUNK : 2 * CHUNK] = chunked(right_low[...])
    left_turn = tn(left_low[...], left_basis[...]).astype(BF)
    right_turn = tn(right_basis[...], right_low[...]).astype(BF)
    half_turned = nn(left_turn, moment_low[...]).astype(BF)
    narrow[:, 2 * CHUNK : 3 * CHUNK] = chunked(nn(half_turned, right_turn).astype(BF))
    narrow_in[me] = narrow[me]
    shift = rotation[0]

    def roll_wide(slot):
        source = (slot + REPLICAS - shift) % REPLICAS
        left = BETA_FACTOR * old_in[source].astype(F32) + weight * outer_in[source].astype(F32)
        return left.astype(BF), wide_in[source]

    def gather_second():
        x_own.wait_recv()
        steps = [pass_on(beside, A, up), pass_on(beside, A, down)]
        to_twin(beside, A)
        b_up.wait_recv()
        steps += [pass_on(down, B0, up), pass_on(down, B, beside)]
        to_twin(down, B)
        b_down.wait_recv()
        steps += [pass_on(up, B1, down), pass_on(up, B, beside)]
        to_twin(up, B)
        a_up.wait_recv()
        steps += [pass_on(down, A0, up)]
        to_twin(down, A)
        a_down.wait_recv()
        steps += [pass_on(up, A1, down)]
        to_twin(up, A)
        x_same.wait_recv()
        to_twin(beside, B)
        return steps

    def gather_third(steps):
        beside_a_up, beside_a_down, b_far0, b_x_down, b_far1, b_x_up, a_far0, a_far1 = steps
        b_far0.wait_recv()
        b_x_far0 = pass_on(far, B0, beside)
        to_twin(far, B0)
        b_far1.wait_recv()
        b_x_far1 = pass_on(far, B1, beside)
        to_twin(far, B1)
        beside_a_up.wait_recv()
        beside_far0 = pass_on(beside_down, A0, up)
        to_twin(beside_down, A)
        beside_a_down.wait_recv()
        beside_far1 = pass_on(beside_up, A1, down)
        to_twin(beside_up, A)
        a_far0.wait_recv()
        to_twin(far, A0)
        a_far1.wait_recv()
        to_twin(far, A1)
        b_x_down.wait_recv()
        to_twin(beside_down, B)
        b_x_up.wait_recv()
        to_twin(beside_up, B)
        return b_x_far0, b_x_far1, beside_far0, beside_far1

    def gather_last(steps):
        for copy, rows in zip(steps, (B0, B1, A0, A1)):
            copy.wait_recv()
            to_twin(beside_far, rows)

    def send_wide(step):
        there = (me + step) % REPLICAS
        left, others = roll_wide(there)
        wide_rolled[there, 0:CHUNK] = left
        wide_rolled[there, CHUNK : 3 * CHUNK] = others
        wide_copy2(step).start()

    def send_narrow(step):
        there = (me + step) % REPLICAS
        narrow_rolled[there] = narrow_in[(there + REPLICAS - shift) % REPLICAS]
        narrow_copy2(step).start()

    each(REPLICAS, lambda step: narrow_copy(step).start())
    second_steps = gather_second()
    for copy in (old_copy, old_copy2, outer_copy, wide_copy):
        each(REPLICAS, lambda step, copy=copy: copy(step).wait_recv())
    each(REPLICAS, send_wide)
    left, others = roll_wide(me)
    wide_out[me, 0:CHUNK] = left
    wide_out[me, CHUNK : 3 * CHUNK] = others
    last_steps = gather_third(second_steps)
    each(REPLICAS, lambda step: narrow_copy(step).wait_recv())
    each(REPLICAS, send_narrow)
    narrow_out[me] = narrow_in[(me + REPLICAS - shift) % REPLICAS]
    gather_last(last_steps)

    for copy in swaps.values():
        copy.wait_send()
    for copy in links:
        copy.wait_send()
    each(REPLICAS, lambda step: ring_copy(step).wait_send())
    each(COLUMNS, lambda step: column_copy(step).wait_send())
    for copy in twins:
        copy.wait()
    for copy in copies:
        copy.wait_send()
    for copy in (old_copy, old_copy2, outer_copy, wide_copy):
        each(REPLICAS, lambda step, copy=copy: copy(step).wait_send())
    each(REPLICAS, lambda step: narrow_copy(step).wait_send())
    each(REPLICAS, lambda step: wide_copy2(step).wait())
    each(REPLICAS, lambda step: narrow_copy2(step).wait())


def step(arrays, rotation):
    hbm = pl.BlockSpec(memory_space=pl.ANY)
    dma = pltpu.SemaphoreType.DMA
    moved = (REPLICAS, 3 * CHUNK, SIDE)

    def block(dtype):
        return pltpu.VMEM((SIDE, SIDE), dtype)

    arrays = [pltpu.with_memory_space_constraint(array, pltpu.HBM) for array in arrays]
    return pl.pallas_call(
        step_kernel,
        out_shape=(
            pltpu.VMEM((REPLICAS, SIDE, SIDE), BF),
            pltpu.VMEM(moved, BF),
            pltpu.VMEM(moved, BF),
        ),
        in_specs=[hbm] * len(arrays) + [pl.BlockSpec(memory_space=pltpu.SMEM)],
        out_specs=(pl.BlockSpec(memory_space=pltpu.VMEM),) * 3,
        scratch_shapes=[
            pltpu.VMEM((8, SIDE, SIDE), BF),
            pltpu.VMEM((8, SIDE, SIDE), BF),
            pltpu.VMEM((4, B_ROWS, SIDE), BF),
            pltpu.VMEM((2, 2, A_HALF, SIDE), BF),
            pltpu.VMEM((2, 2, A_ROWS, SIDE), BF),
            pltpu.VMEM((2, B_HALF, SIDE), BF),
            pltpu.VMEM((2, B_ROWS, SIDE), BF),
            pltpu.VMEM((A_ROWS, SIDE), BF),
            pltpu.VMEM((REPLICAS, 8, 128), F32),
            pltpu.VMEM((COLUMNS, 8, 128), F32),
            block(F32),
            block(F32),
            block(F32),
            block(BF),
            block(BF),
            block(BF),
            block(BF),
            block(BF),
            block(F32),
            block(BF),
            block(F32),
            block(F32),
            block(BF),
            block(BF),
            block(BF),
            block(BF),
        ]
        + [block(BF)]
        + [pltpu.VMEM((REPLICAS, CHUNK, SIDE), BF)] * 4
        + [pltpu.VMEM((REPLICAS, 2 * CHUNK, SIDE), BF)] * 2
        + [pltpu.VMEM(moved, BF)] * 4
        + [dma((8,)), dma((7,)), dma((8,)), dma((8,)), dma((23,)), dma((23,))]
        + [dma((REPLICAS,))] * 2
        + [dma((COLUMNS,))] * 2
        + [dma((18,))] * 2
        + [dma((19,))] * 2
        + [dma((REPLICAS,))] * 14,
        compiler_params=pltpu.CompilerParams(
            collective_id=0, has_side_effects=True, vmem_limit_bytes=46 * 2**20
        ),
        cost_estimate=pl.CostEstimate(
            flops=10**10, bytes_accessed=32 * 2**20, transcendentals=0
        ),
        name="soap_step",
    )(*arrays, rotation)


def finish_kernel(params, wide, narrow, params_out, left, right, second, *rest):
    left_basis, right_basis, first, staged, sems = rest
    copies = [pltpu.make_async_copy(params, params_out, sems.at[0])]
    for k, target in enumerate((left_basis, right_basis, first)):
        copies.append(
            pltpu.make_async_copy(
                narrow.at[:, pl.ds(CHUNK * k, CHUNK)], target, sems.at[1 + k]
            )
        )
    for copy in copies:
        copy.start()
    for k, target in enumerate((left, right, second)):
        staged[k] = wide[:, CHUNK * k : CHUNK * (k + 1)].astype(F32)
        copies.append(pltpu.make_async_copy(staged.at[k], target, sems.at[4 + k]))
        copies[-1].start()
    for copy in copies:
        copy.wait()


def finish(params, wide, narrow):
    hbm = pl.BlockSpec(memory_space=pl.ANY)
    vmem = pl.BlockSpec(memory_space=pltpu.VMEM)
    slots = (REPLICAS, CHUNK, SIDE)
    return pl.pallas_call(
        finish_kernel,
        out_shape=(pltpu.HBM((REPLICAS, SIDE, SIDE), BF),)
        + (pltpu.HBM(slots, F32),) * 3
        + (pltpu.HBM(slots, BF),) * 3,
        in_specs=[vmem, vmem, vmem],
        out_specs=(hbm,) * 7,
        scratch_shapes=[
            pltpu.VMEM((3,) + slots, F32),
            pltpu.SemaphoreType.DMA((7,)),
        ],
        compiler_params=pltpu.CompilerParams(vmem_limit_bytes=24 * 2**20),
        cost_estimate=pl.CostEstimate(flops=0, bytes_accessed=24 * 2**20, transcendentals=0),
        name="finish",
    )(params, wide, narrow)


def local(
    grads,
    left_factor,
    right_factor,
    left_basis,
    right_basis,
    first_moment,
    second_moment,
    parameters,
    rotation,
):
    blocks = (
        left_factor,
        right_factor,
        second_moment,
        left_basis,
        right_basis,
        first_moment,
        parameters,
    )
    params, wide, narrow = step([grads[0, :, 0]] + [value[0, 0] for value in blocks], rotation)
    gathered, *outs = finish(params, wide, narrow)
    left, right, second, left_turned, right_turned, first = (
        value.reshape(1, 1, SIDE, SIDE) for value in outs
    )
    return (gathered[:, None], left, right, left_turned, right_turned, first, second)


def solution(mesh):
    state = P("dp", "fsdp", None, None)
    return jax.shard_map(
        local,
        mesh=mesh,
        in_specs=(P("dp", None, "fsdp", None, None),) + (state,) * 7 + (P("fsdp"),),
        out_specs=(P(None, "fsdp", None, None),) + (state,) * 6,
        check_vma=False,
    )
```

```python
import math

import jax
import jax.numpy as jnp
from jax import lax
from jax.experimental import pallas as pl
from jax.experimental.pallas import tpu as pltpu
from jax.sharding import PartitionSpec as P

ITERS = 2
NEWTON = 3
SIDE = 512
REPLICAS = 16
COLUMNS = 8
CHUNK = SIDE // REPLICAS

BETA_MOMENT = 0.95
BETA_SECOND = 0.95
BETA_FACTOR = 0.95
STEP_RATE = 0.05
CLIP_RMS = 0.3
TINY = 1e-08

A_HALF = 144
A_ROWS = 2 * A_HALF
B_ROWS = SIDE - A_ROWS
B_HALF = B_ROWS // 2
A = pl.ds(0, A_ROWS)
B = pl.ds(A_ROWS, B_ROWS)
A0, A1 = pl.ds(0, A_HALF), pl.ds(A_HALF, A_HALF)
B0, B1 = pl.ds(A_ROWS, B_HALF), pl.ds(A_ROWS + B_HALF, B_HALF)
LATE0, LATE1 = pl.ds(0, B_HALF), pl.ds(B_HALF, B_HALF)

MESH = pl.DeviceIdType.MESH
BF = jnp.bfloat16
F32 = jnp.float32


def place():
    me = lax.axis_index("dp")
    return me, me // 4, me // 2 % 2, me % 2


def index_of(y, x, core):
    return y % 4 * 4 + x % 2 * 2 + core % 2


def remote(src, dst, send, recv, **where):
    return pltpu.make_async_remote_copy(
        src_ref=src, dst_ref=dst, send_sem=send, recv_sem=recv, device_id=where, device_id_type=MESH
    )


def greet_replicas(barrier, me):
    def greet(step, carry):
        pl.semaphore_signal(
            barrier, inc=1, device_id={"dp": (me + step) % REPLICAS}, device_id_type=MESH
        )
        return carry

    lax.fori_loop(1, REPLICAS, greet, 0)


def nn(a, b):
    return jnp.dot(a, b, preferred_element_type=F32)


def nt(a, b):
    return lax.dot_general(a, b, (((1,), (1,)), ((), ())), preferred_element_type=F32)


def tn(a, b):
    return lax.dot_general(a, b, (((0,), (0,)), ((), ())), preferred_element_type=F32)


def each(count, act):
    lax.fori_loop(1, count, lambda step, carry: (act(step), carry)[1], 0)


def chunked(value):
    return value.reshape(REPLICAS, CHUNK, SIDE)


def image_step(factor, basis, iterate, low):
    image = nn(factor, basis)
    magnitude = jnp.abs(image)
    bound = (
        jnp.sqrt(jnp.max(jnp.sum(magnitude, axis=0)) * jnp.max(jnp.sum(magnitude, axis=1)))
        + 1e-06
    )
    scaled = image * (1.0 / bound)
    iterate[...] = scaled
    low[...] = scaled.astype(BF)


def newton_step(iterate, low, gram):
    gram[...] = nt(low[...], low[...]).astype(BF)
    value = 1.5 * iterate[...] - 0.5 * nn(gram[...], low[...])
    iterate[...] = value
    low[...] = value.astype(BF)


def step_kernel(
    grads,
    left_hbm,
    right_hbm,
    second_hbm,
    left_basis_hbm,
    right_basis_hbm,
    first_hbm,
    param_hbm,
    rotation,
    params_out,
    wide_out,
    second_out,
    left_low,
    right_low,
    first_out,
    own,
    twin,
    x_in,
    y_relay,
    y_in,
    late_relay,
    y_late,
    x_late,
    tile,
    tile2,
    left_old,
    right_old,
    second_old,
    left_basis,
    right_basis,
    first_old,
    param_old,
    grad_low,
    rotated,
    left_iter,
    right_iter,
    left_gram,
    right_gram,
    wide,
    wide_in,
    wide_rolled,
    left_in,
    left_rolled,
    left_moved,
    right_in,
    right_rolled,
    right_moved,
    second,
    second_in,
    second_rolled,
    local_sem,
    load_sem,
    core_send,
    core_recv,
    send,
    recv,
    ring_send,
    ring_recv,
    column_send,
    column_recv,
    ag_send,
    ag_recv,
    twin_send,
    twin_recv,
    wide_send,
    wide_recv,
    wide_send2,
    wide_recv2,
    second_send,
    second_recv,
    second_send2,
    second_recv2,
    left_send,
    left_recv,
    left_send2,
    left_recv2,
    right_send,
    right_recv,
    right_send2,
    right_recv2,
):
    me, y, x, core = place()
    column = lax.axis_index("fsdp")
    barrier = pltpu.get_barrier_semaphore()
    greet_replicas(barrier, me)
    def greet_column(step, carry):
        pl.semaphore_signal(
            barrier, inc=1, device_id={"fsdp": (column + step) % COLUMNS}, device_id_type=MESH
        )
        return carry

    lax.fori_loop(1, COLUMNS, greet_column, 0)

    beside = index_of(y, x + 1, core)
    other = index_of(y, x, core + 1)
    up = index_of(y + 1, x, core)
    down = index_of(y - 1, x, core)
    order = [(2, 1), (2, 0), (1, 1), (3, 1), (1, 0), (3, 0), (0, 1), (0, 0)]
    loads, swaps = {}, {}
    for dy, dx in order:
        k = dy * 2 + dx
        loads[dy, dx] = pltpu.make_async_copy(
            grads.at[index_of(y + dy, x + dx, core)], own.at[k], local_sem.at[k]
        )
        loads[dy, dx].start()
    pl.semaphore_wait(barrier, REPLICAS - 1 + COLUMNS - 1)
    for dy, dx in order:
        k = dy * 2 + dx
        swaps[dy, dx] = remote(
            grads.at[index_of(y + dy, x + dx, core + 1)],
            twin.at[k],
            core_send.at[k],
            core_recv.at[k],
            dp=other,
        )
        swaps[dy, dx].start()

    state_loads = [
        pltpu.make_async_copy(source, target, load_sem.at[k])
        for k, (source, target) in enumerate(
            (
                (left_basis_hbm, left_basis),
                (right_basis_hbm, right_basis),
                (first_hbm, first_old),
                (second_hbm, second_old),
                (left_hbm, left_old),
                (right_hbm, right_old),
                (param_hbm, param_old),
            )
        )
    ]
    for load in state_loads:
        load.start()

    shift = rotation[0]

    def state_copy(source, target, sends, recvs, step):
        there = (me + step) % REPLICAS
        return remote(
            source.at[there], target.at[me], sends.at[step], recvs.at[step], dp=there
        )

    def send_rolled(source, rolled, target, copy):
        def one(step):
            there = (me + step) % REPLICAS
            rolled[there] = source[(there + REPLICAS - shift) % REPLICAS]
            copy(step).start()

        each(REPLICAS, one)
        target[me] = source[(me + REPLICAS - shift) % REPLICAS]

    def left_copy(step):
        return state_copy(left_basis_hbm, left_in, left_send, left_recv, step)

    def left_copy2(step):
        return state_copy(left_rolled, left_moved, left_send2, left_recv2, step)

    def right_copy(step):
        return state_copy(right_basis_hbm, right_in, right_send, right_recv, step)

    def right_copy2(step):
        return state_copy(right_rolled, right_moved, right_send2, right_recv2, step)

    def wide_copy(step):
        return state_copy(wide, wide_in, wide_send, wide_recv, step)

    def wide_copy2(step):
        return state_copy(wide_rolled, wide_out, wide_send2, wide_recv2, step)

    def second_copy(step):
        return state_copy(second, second_in, second_send, second_recv, step)

    def second_copy2(step):
        return state_copy(second_rolled, second_out, second_send2, second_recv2, step)

    each(REPLICAS, lambda step: left_copy(step).start())

    links = []

    def link(source, target, device):
        k = len(links)
        copy = remote(source, target, send.at[k], recv.at[k], dp=device)
        copy.start()
        links.append(copy)
        return copy

    def add(k, rows, value):
        own[k, rows] = own[k, rows] + value

    x_first, far_up, far_down, free_up, free_down, near_up, near_down = ({} for _ in range(7))
    for dy, dx in order:
        k = dy * 2 + dx
        loads[dy, dx].wait()
        swaps[dy, dx].wait_recv()
        own[k] = own[k] + twin[k]
        if dx == 1:
            x_first[dy] = link(own.at[k, B], x_in.at[dy], beside)
        if dy == 2:
            far_up[dx] = link(own.at[k, A0], y_relay.at[0, dx], up)
            far_down[dx] = link(own.at[k, A1], y_relay.at[1, dx], down)
        if dy == 1:
            free_up[dx] = link(own.at[k, A1], y_in.at[0, dx, A1], up)
        if dy == 3:
            free_down[dx] = link(own.at[k, A0], y_in.at[1, dx, A0], down)

    def relay_rows(dx):
        far_up[dx].wait_recv()
        add(2 + dx, A0, y_relay[0, dx])
        near_up[dx] = link(own.at[2 + dx, A0], y_in.at[0, dx, A0], up)
        far_down[dx].wait_recv()
        add(6 + dx, A1, y_relay[1, dx])
        near_down[dx] = link(own.at[6 + dx, A1], y_in.at[1, dx, A1], down)

    relay_rows(1)
    x_first[2].wait_recv()
    add(4, B, x_in[2])
    late_far_up = link(own.at[4, B0], late_relay.at[0], up)
    late_far_down = link(own.at[4, B1], late_relay.at[1], down)
    relay_rows(0)
    x_first[1].wait_recv()
    add(2, B, x_in[1])
    late_free_up = link(own.at[2, B1], y_late.at[0, LATE1], up)
    x_first[3].wait_recv()
    add(6, B, x_in[3])
    late_free_down = link(own.at[6, B0], y_late.at[1, LATE0], down)
    for group in (free_up, near_up, free_down, near_down):
        group[1].wait_recv()
    own[1, A] = (
        own[1, A].astype(F32) + (y_in[0, 1].astype(F32) + y_in[1, 1].astype(F32))
    ).astype(BF)
    x_second = link(own.at[1, A], x_late, beside)
    late_far_up.wait_recv()
    add(2, B0, late_relay[0])
    late_near_up = link(own.at[2, B0], y_late.at[0, LATE0], up)
    late_far_down.wait_recv()
    add(6, B1, late_relay[1])
    late_near_down = link(own.at[6, B1], y_late.at[1, LATE1], down)
    each(REPLICAS, lambda step: right_copy(step).start())
    for group in (free_up, near_up, free_down, near_down):
        group[0].wait_recv()
    x_first[0].wait_recv()
    x_second.wait_recv()
    mean_y = (
        (own[0, A].astype(F32) + x_late[...].astype(F32))
        + (y_in[0, 0].astype(F32) + y_in[1, 0].astype(F32))
    ) * (1.0 / REPLICAS)
    grad_low[A] = mean_y.astype(BF)
    for copy in (late_free_up, late_near_up, late_free_down, late_near_down):
        copy.wait_recv()
    mean_x = (
        (own[0, B].astype(F32) + x_in[0].astype(F32))
        + (y_late[0].astype(F32) + y_late[1].astype(F32))
    ) * (1.0 / REPLICAS)
    grad_low[B] = mean_x.astype(BF)
    squares = jnp.sum((mean_x * mean_x).reshape(B_ROWS // 8, 8, SIDE), axis=0) + jnp.sum(
        (mean_y * mean_y).reshape(A_ROWS // 8, 8, SIDE), axis=0
    )
    tile2[0] = (squares[:, :128] + squares[:, 128:256]) + (squares[:, 256:384] + squares[:, 384:])

    def ring_copy(step):
        return remote(
            tile.at[0],
            tile.at[step],
            ring_send.at[step],
            ring_recv.at[step],
            dp=(me + step) % REPLICAS,
        )

    def column_copy(step):
        return remote(
            tile2.at[0],
            tile2.at[step],
            column_send.at[step],
            column_recv.at[step],
            fsdp=(column + step) % COLUMNS,
        )

    each(COLUMNS, lambda step: column_copy(step).start())
    for load in state_loads:
        load.wait()
    left_in[me] = left_basis[me]
    right_in[me] = right_basis[me]
    left_start = left_basis[...].reshape(SIDE, SIDE)
    right_start = right_basis[...].reshape(SIDE, SIDE)
    half_left = tn(left_start, grad_low[...]).astype(BF)
    rotated[...] = nn(half_left, right_start)
    each(COLUMNS, lambda step: column_copy(step).wait_recv())
    tile[0] = jnp.sum(tile2[...], axis=0)
    each(REPLICAS, lambda step: ring_copy(step).start())
    each(REPLICAS, lambda step: left_copy(step).wait_recv())
    send_rolled(left_in, left_rolled, left_moved, left_copy2)
    left_iter[...] = nt(grad_low[...], grad_low[...])
    right_iter[...] = tn(grad_low[...], grad_low[...])
    each(REPLICAS, lambda step: right_copy(step).wait_recv())
    send_rolled(right_in, right_rolled, right_moved, right_copy2)
    each(REPLICAS, lambda step: ring_copy(step).wait_recv())
    square_sum = jnp.sum(jnp.sum(tile[...], axis=0))
    entries = SIDE * SIDE * REPLICAS * COLUMNS
    clip_factor = jnp.minimum(1.0, CLIP_RMS * math.sqrt(entries) / jnp.sqrt(square_sum + 1e-06))

    weight = (1.0 - BETA_FACTOR) * (clip_factor * clip_factor)
    turned = clip_factor * rotated[...]
    moment = BETA_MOMENT * first_old[...].astype(F32) + (1.0 - BETA_MOMENT) * turned
    wide[:, 2 * CHUNK : 3 * CHUNK] = chunked(moment.astype(BF))
    left_new = (BETA_FACTOR * left_old[...] + weight * left_iter[...]).astype(BF)
    right_new = (BETA_FACTOR * right_old[...] + weight * right_iter[...]).astype(BF)
    wide[:, 0:CHUNK] = chunked(left_new)
    wide[:, CHUNK : 2 * CHUNK] = chunked(right_new)
    each(REPLICAS, lambda step: wide_copy(step).start())
    wide_in[me] = wide[me]
    second_new = BETA_SECOND * second_old[...] + (1.0 - BETA_SECOND) * turned * turned
    second[...] = chunked(second_new.astype(BF))
    second_in[me] = second[me]
    direction = (moment / (jnp.sqrt(second_new) + TINY)).astype(BF)
    half_back = nn(left_basis[...].reshape(SIDE, SIDE), direction).astype(BF)
    update = nt(half_back, right_basis[...].reshape(SIDE, SIDE))
    params_out[me] = (param_old[...].astype(F32) - STEP_RATE * update).astype(BF)

    far = index_of(y + 2, x, core)
    beside_down = index_of(y - 1, x + 1, core)
    beside_up = index_of(y + 1, x + 1, core)
    beside_far = index_of(y + 2, x + 1, core)
    copies, twins = [], []

    def pass_on(owner, rows, target):
        k = len(copies)
        view = params_out.at[owner, rows]
        copy = remote(view, view, ag_send.at[k], ag_recv.at[k], dp=target)
        copy.start()
        copies.append(copy)
        return copy

    def to_twin(owner, rows):
        k = len(twins)
        view = params_out.at[owner, rows]
        copy = remote(view, view, twin_send.at[k], twin_recv.at[k], dp=other)
        copy.start()
        twins.append(copy)

    x_own = pass_on(me, A, beside)
    b_up = pass_on(me, B, up)
    b_down = pass_on(me, B, down)
    a_up = pass_on(me, A, up)
    a_down = pass_on(me, A, down)
    x_same = pass_on(me, B, beside)
    to_twin(me, pl.ds(0, SIDE))

    def gather_second():
        x_own.wait_recv()
        steps = [pass_on(beside, A, up), pass_on(beside, A, down)]
        to_twin(beside, A)
        b_up.wait_recv()
        steps += [pass_on(down, B0, up), pass_on(down, B, beside)]
        to_twin(down, B)
        b_down.wait_recv()
        steps += [pass_on(up, B1, down), pass_on(up, B, beside)]
        to_twin(up, B)
        a_up.wait_recv()
        steps += [pass_on(down, A0, up)]
        to_twin(down, A)
        a_down.wait_recv()
        steps += [pass_on(up, A1, down)]
        to_twin(up, A)
        x_same.wait_recv()
        to_twin(beside, B)
        return steps

    def gather_third(steps):
        beside_a_up, beside_a_down, b_far0, b_x_down, b_far1, b_x_up, a_far0, a_far1 = steps
        b_far0.wait_recv()
        b_x_far0 = pass_on(far, B0, beside)
        to_twin(far, B0)
        b_far1.wait_recv()
        b_x_far1 = pass_on(far, B1, beside)
        to_twin(far, B1)
        beside_a_up.wait_recv()
        beside_far0 = pass_on(beside_down, A0, up)
        to_twin(beside_down, A)
        beside_a_down.wait_recv()
        beside_far1 = pass_on(beside_up, A1, down)
        to_twin(beside_up, A)
        a_far0.wait_recv()
        to_twin(far, A0)
        a_far1.wait_recv()
        to_twin(far, A1)
        b_x_down.wait_recv()
        to_twin(beside_down, B)
        b_x_up.wait_recv()
        to_twin(beside_up, B)
        return b_x_far0, b_x_far1, beside_far0, beside_far1

    def gather_last(steps):
        for copy, rows in zip(steps, (B0, B1, A0, A1)):
            copy.wait_recv()
            to_twin(beside_far, rows)

    each(REPLICAS, lambda step: wide_copy(step).wait_recv())
    send_rolled(wide_in, wide_rolled, wide_out, wide_copy2)
    second_steps = gather_second()
    each(REPLICAS, lambda step: second_copy(step).start())

    for copy in (left_copy2, right_copy2, wide_copy2):
        each(REPLICAS, lambda step, copy=copy: copy(step).wait_recv())
    left_start = left_moved[...].reshape(SIDE, SIDE)
    right_start = right_moved[...].reshape(SIDE, SIDE)
    for repeat in range(ITERS):
        image_step(
            wide_out[:, 0:CHUNK].reshape(SIDE, SIDE),
            left_start if repeat == 0 else left_low[...],
            left_iter,
            left_low,
        )
        image_step(
            wide_out[:, CHUNK : 2 * CHUNK].reshape(SIDE, SIDE),
            right_start if repeat == 0 else right_low[...],
            right_iter,
            right_low,
        )
        for newton in range(NEWTON):
            newton_step(left_iter, left_low, left_gram)
            newton_step(right_iter, right_low, right_gram)
    left_turn = tn(left_low[...], left_start).astype(BF)
    right_turn = tn(right_start, right_low[...]).astype(BF)
    moment_low = wide_out[:, 2 * CHUNK : 3 * CHUNK].reshape(SIDE, SIDE)
    half_turned = nn(left_turn, moment_low).astype(BF)
    first_out[...] = nn(half_turned, right_turn).astype(BF)

    last_steps = gather_third(second_steps)
    each(REPLICAS, lambda step: second_copy(step).wait_recv())
    send_rolled(second_in, second_rolled, second_out, second_copy2)
    gather_last(last_steps)

    for copy in swaps.values():
        copy.wait_send()
    for copy in links:
        copy.wait_send()
    each(REPLICAS, lambda step: ring_copy(step).wait_send())
    each(COLUMNS, lambda step: column_copy(step).wait_send())
    for copy in twins:
        copy.wait()
    for copy in copies:
        copy.wait_send()
    for copy in (left_copy, right_copy, wide_copy, second_copy, left_copy2, right_copy2, wide_copy2):
        each(REPLICAS, lambda step, copy=copy: copy(step).wait_send())
    each(REPLICAS, lambda step: second_copy2(step).wait())


def step(arrays, rotation):
    hbm = pl.BlockSpec(memory_space=pl.ANY)
    dma = pltpu.SemaphoreType.DMA
    slots = (REPLICAS, CHUNK, SIDE)
    moved = (REPLICAS, 3 * CHUNK, SIDE)

    def block(dtype):
        return pltpu.VMEM((SIDE, SIDE), dtype)

    arrays = [pltpu.with_memory_space_constraint(array, pltpu.HBM) for array in arrays]
    return pl.pallas_call(
        step_kernel,
        out_shape=(
            pltpu.VMEM((REPLICAS, SIDE, SIDE), BF),
            pltpu.VMEM(moved, BF),
            pltpu.VMEM(slots, BF),
            block(BF),
            block(BF),
            block(BF),
        ),
        in_specs=[hbm] * len(arrays) + [pl.BlockSpec(memory_space=pltpu.SMEM)],
        out_specs=(pl.BlockSpec(memory_space=pltpu.VMEM),) * 6,
        scratch_shapes=[
            pltpu.VMEM((8, SIDE, SIDE), BF),
            pltpu.VMEM((8, SIDE, SIDE), BF),
            pltpu.VMEM((4, B_ROWS, SIDE), BF),
            pltpu.VMEM((2, 2, A_HALF, SIDE), BF),
            pltpu.VMEM((2, 2, A_ROWS, SIDE), BF),
            pltpu.VMEM((2, B_HALF, SIDE), BF),
            pltpu.VMEM((2, B_ROWS, SIDE), BF),
            pltpu.VMEM((A_ROWS, SIDE), BF),
            pltpu.VMEM((REPLICAS, 8, 128), F32),
            pltpu.VMEM((COLUMNS, 8, 128), F32),
            block(F32),
            block(F32),
            block(F32),
            pltpu.VMEM(slots, BF),
            pltpu.VMEM(slots, BF),
            block(BF),
            block(BF),
            block(BF),
            block(F32),
            block(F32),
            block(F32),
            block(BF),
            block(BF),
        ]
        + [pltpu.VMEM(moved, BF)] * 3
        + [pltpu.VMEM(slots, BF)] * 9
        + [dma((8,)), dma((7,)), dma((8,)), dma((8,)), dma((23,)), dma((23,))]
        + [dma((REPLICAS,))] * 2
        + [dma((COLUMNS,))] * 2
        + [dma((18,))] * 2
        + [dma((19,))] * 2
        + [dma((REPLICAS,))] * 16,
        compiler_params=pltpu.CompilerParams(
            collective_id=0, has_side_effects=True, vmem_limit_bytes=46 * 2**20
        ),
        cost_estimate=pl.CostEstimate(
            flops=10**10, bytes_accessed=32 * 2**20, transcendentals=0
        ),
        name="soap_step",
    )(*arrays, rotation)


def finish_kernel(
    params,
    wide,
    second,
    left_low,
    right_low,
    first,
    params_out,
    left_out,
    right_out,
    second_out,
    left_basis_out,
    right_basis_out,
    first_out,
    staged,
    sems,
):
    copies = [
        pltpu.make_async_copy(source, target, sems.at[k])
        for k, (source, target) in enumerate(
            (
                *(
                    (params.at[pl.ds(4 * part, 4)], params_out.at[pl.ds(4 * part, 4)])
                    for part in range(4)
                ),
                (left_low, left_basis_out),
                (right_low, right_basis_out),
                (first, first_out),
            )
        )
    ]
    for copy in copies:
        copy.start()
    for k, target in enumerate((left_out, right_out, second_out)):
        source = second[...] if k == 2 else wide[:, CHUNK * k : CHUNK * (k + 1)]
        staged[k] = source.astype(F32)
        copies.append(pltpu.make_async_copy(staged.at[k], target, sems.at[7 + k]))
        copies[-1].start()
    for copy in copies:
        copy.wait()


def finish(arrays):
    slots = (REPLICAS, CHUNK, SIDE)
    return pl.pallas_call(
        finish_kernel,
        out_shape=(pltpu.HBM((REPLICAS, SIDE, SIDE), BF),)
        + (pltpu.HBM(slots, F32),) * 3
        + (pltpu.HBM((SIDE, SIDE), BF),) * 3,
        in_specs=[pl.BlockSpec(memory_space=pltpu.VMEM)] * len(arrays),
        out_specs=(pl.BlockSpec(memory_space=pl.ANY),) * 7,
        scratch_shapes=[
            pltpu.VMEM((3,) + slots, F32),
            pltpu.SemaphoreType.DMA((10,)),
        ],
        compiler_params=pltpu.CompilerParams(vmem_limit_bytes=24 * 2**20),
        cost_estimate=pl.CostEstimate(flops=0, bytes_accessed=24 * 2**20, transcendentals=0),
        name="finish",
    )(*arrays)


def local(
    grads,
    left_factor,
    right_factor,
    left_basis,
    right_basis,
    first_moment,
    second_moment,
    parameters,
    rotation,
):
    blocks = (
        left_factor,
        right_factor,
        second_moment,
        left_basis,
        right_basis,
        first_moment,
        parameters,
    )
    slots = (REPLICAS, CHUNK, SIDE)
    arrays = [grads[0, :, 0]] + [value[0, 0] for value in blocks]
    for k in (4, 5):
        arrays[k] = arrays[k].reshape(slots)
    gathered, *outs = finish(step(arrays, rotation))
    left, right, second, left_turned, right_turned, first = (
        value.reshape(1, 1, SIDE, SIDE) for value in outs
    )
    return (gathered[:, None], left, right, left_turned, right_turned, first, second)


def solution(mesh):
    state = P("dp", "fsdp", None, None)
    return jax.shard_map(
        local,
        mesh=mesh,
        in_specs=(P("dp", None, "fsdp", None, None),) + (state,) * 7 + (P("fsdp"),),
        out_specs=(P(None, "fsdp", None, None),) + (state,) * 6,
        check_vma=False,
    )
```

```python
import math

import jax
import jax.numpy as jnp
from jax import lax
from jax.experimental import pallas as pl
from jax.experimental.pallas import tpu as pltpu
from jax.sharding import PartitionSpec as P

ITERS = 2
NEWTON = 3
SIDE = 512
REPLICAS = 16
COLUMNS = 8
CHUNK = SIDE // REPLICAS

BETA_MOMENT = 0.95
BETA_SECOND = 0.95
BETA_FACTOR = 0.95
STEP_RATE = 0.05
CLIP_RMS = 0.3
TINY = 1e-08

A_HALF = 144
A_ROWS = 2 * A_HALF
B_ROWS = SIDE - A_ROWS
B_HALF = B_ROWS // 2
A = pl.ds(0, A_ROWS)
B = pl.ds(A_ROWS, B_ROWS)
A0, A1 = pl.ds(0, A_HALF), pl.ds(A_HALF, A_HALF)
B0, B1 = pl.ds(A_ROWS, B_HALF), pl.ds(A_ROWS + B_HALF, B_HALF)
LATE0, LATE1 = pl.ds(0, B_HALF), pl.ds(B_HALF, B_HALF)

MESH = pl.DeviceIdType.MESH
BF = jnp.bfloat16
F32 = jnp.float32


def place():
    me = lax.axis_index("dp")
    return me, me // 4, me // 2 % 2, me % 2


def index_of(y, x, core):
    return y % 4 * 4 + x % 2 * 2 + core % 2


def remote(src, dst, send, recv, **where):
    return pltpu.make_async_remote_copy(
        src_ref=src, dst_ref=dst, send_sem=send, recv_sem=recv, device_id=where, device_id_type=MESH
    )


def greet_replicas(barrier, me):
    def greet(step, carry):
        pl.semaphore_signal(
            barrier, inc=1, device_id={"dp": (me + step) % REPLICAS}, device_id_type=MESH
        )
        return carry

    lax.fori_loop(1, REPLICAS, greet, 0)


def nn(a, b):
    return jnp.dot(a, b, preferred_element_type=F32)


def nt(a, b):
    return lax.dot_general(a, b, (((1,), (1,)), ((), ())), preferred_element_type=F32)


def tn(a, b):
    return lax.dot_general(a, b, (((0,), (0,)), ((), ())), preferred_element_type=F32)


def each(count, act):
    lax.fori_loop(1, count, lambda step, carry: (act(step), carry)[1], 0)


def chunked(value):
    return value.reshape(REPLICAS, CHUNK, SIDE)


def image_step(factor, basis, iterate, low):
    image = nn(factor, basis)
    magnitude = jnp.abs(image)
    bound = (
        jnp.sqrt(jnp.max(jnp.sum(magnitude, axis=0)) * jnp.max(jnp.sum(magnitude, axis=1)))
        + 1e-06
    )
    scaled = image * (1.0 / bound)
    iterate[...] = scaled
    low[...] = scaled.astype(BF)


def newton_step(iterate, low, gram):
    gram[...] = nt(low[...], low[...]).astype(BF)
    value = 1.5 * iterate[...] - 0.5 * nn(gram[...], low[...])
    iterate[...] = value
    low[...] = value.astype(BF)


def step_kernel(
    grads,
    left_hbm,
    right_hbm,
    second_hbm,
    left_basis_hbm,
    right_basis_hbm,
    first_hbm,
    param_hbm,
    rotation,
    params_out,
    wide_out,
    second_out,
    left_low,
    right_low,
    first_out,
    own,
    twin,
    x_in,
    y_relay,
    y_in,
    late_relay,
    y_late,
    x_late,
    tile,
    tile2,
    left_old,
    right_old,
    second_old,
    left_basis,
    right_basis,
    first_old,
    param_old,
    grad_low,
    rotated,
    left_iter,
    right_iter,
    left_gram,
    right_gram,
    wide,
    wide_in,
    wide_rolled,
    left_in,
    left_rolled,
    left_moved,
    right_in,
    right_rolled,
    right_moved,
    second,
    second_in,
    second_rolled,
    local_sem,
    load_sem,
    core_send,
    core_recv,
    send,
    recv,
    ring_send,
    ring_recv,
    column_send,
    column_recv,
    ag_send,
    ag_recv,
    twin_send,
    twin_recv,
    wide_send,
    wide_recv,
    wide_send2,
    wide_recv2,
    second_send,
    second_recv,
    second_send2,
    second_recv2,
    left_late_send,
    left_late_recv,
    left_send,
    left_recv,
    left_send2,
    left_recv2,
    right_late_send,
    right_late_recv,
    right_send,
    right_recv,
    right_send2,
    right_recv2,
):
    me, y, x, core = place()
    column = lax.axis_index("fsdp")
    barrier = pltpu.get_barrier_semaphore()
    greet_replicas(barrier, me)
    def greet_column(step, carry):
        pl.semaphore_signal(
            barrier, inc=1, device_id={"fsdp": (column + step) % COLUMNS}, device_id_type=MESH
        )
        return carry

    lax.fori_loop(1, COLUMNS, greet_column, 0)

    beside = index_of(y, x + 1, core)
    other = index_of(y, x, core + 1)
    up = index_of(y + 1, x, core)
    down = index_of(y - 1, x, core)
    order = [(2, 1), (2, 0), (1, 1), (3, 1), (1, 0), (3, 0), (0, 1), (0, 0)]
    loads, swaps = {}, {}
    for dy, dx in order:
        k = dy * 2 + dx
        loads[dy, dx] = pltpu.make_async_copy(
            grads.at[index_of(y + dy, x + dx, core)], own.at[k], local_sem.at[k]
        )
        loads[dy, dx].start()
    pl.semaphore_wait(barrier, REPLICAS - 1 + COLUMNS - 1)
    for dy, dx in order:
        k = dy * 2 + dx
        swaps[dy, dx] = remote(
            grads.at[index_of(y + dy, x + dx, core + 1)],
            twin.at[k],
            core_send.at[k],
            core_recv.at[k],
            dp=other,
        )
        swaps[dy, dx].start()

    state_loads = [
        pltpu.make_async_copy(source, target, load_sem.at[k])
        for k, (source, target) in enumerate(
            (
                (left_basis_hbm, left_basis),
                (right_basis_hbm, right_basis),
                (first_hbm, first_old),
                (second_hbm, second_old),
                (left_hbm, left_old),
                (right_hbm, right_old),
                (param_hbm, param_old),
            )
        )
    ]
    for load in state_loads:
        load.start()

    shift = rotation[0]

    def state_copy(source, target, sends, recvs, step):
        there = (me + step) % REPLICAS
        return remote(
            source.at[there], target.at[me], sends.at[step], recvs.at[step], dp=there
        )

    def send_rolled(source, rolled, target, copy):
        def one(step):
            there = (me + step) % REPLICAS
            rolled[there] = source[(there + REPLICAS - shift) % REPLICAS]
            copy(step).start()

        each(REPLICAS, one)
        target[me] = source[(me + REPLICAS - shift) % REPLICAS]

    def half_copy(source, target, start, sends, recvs, step):
        there = (me + step) % REPLICAS
        rows = pl.ds(start, CHUNK // 2)
        return remote(
            source.at[there, rows], target.at[me, rows], sends.at[step], recvs.at[step], dp=there
        )

    def left_copy(step):
        return half_copy(left_basis_hbm, left_in, 0, left_send, left_recv, step)

    def left_late(step):
        return half_copy(
            left_basis_hbm, left_in, CHUNK // 2, left_late_send, left_late_recv, step
        )

    def left_copy2(step):
        return state_copy(left_rolled, left_moved, left_send2, left_recv2, step)

    def right_copy(step):
        return half_copy(right_basis_hbm, right_in, 0, right_send, right_recv, step)

    def right_late(step):
        return half_copy(
            right_basis_hbm, right_in, CHUNK // 2, right_late_send, right_late_recv, step
        )

    def right_copy2(step):
        return state_copy(right_rolled, right_moved, right_send2, right_recv2, step)

    def wide_copy(step):
        return state_copy(wide, wide_in, wide_send, wide_recv, step)

    def wide_copy2(step):
        return state_copy(wide_rolled, wide_out, wide_send2, wide_recv2, step)

    def second_copy(step):
        return state_copy(second, second_in, second_send, second_recv, step)

    def second_copy2(step):
        return state_copy(second_rolled, second_out, second_send2, second_recv2, step)

    each(REPLICAS, lambda step: left_copy(step).start())

    links = []

    def link(source, target, device):
        k = len(links)
        copy = remote(source, target, send.at[k], recv.at[k], dp=device)
        copy.start()
        links.append(copy)
        return copy

    def add(k, rows, value):
        own[k, rows] = own[k, rows] + value

    x_first, far_up, far_down, free_up, free_down, near_up, near_down = ({} for _ in range(7))
    for dy, dx in order:
        k = dy * 2 + dx
        loads[dy, dx].wait()
        swaps[dy, dx].wait_recv()
        own[k] = own[k] + twin[k]
        if dx == 1:
            x_first[dy] = link(own.at[k, B], x_in.at[dy], beside)
        if dy == 2:
            far_up[dx] = link(own.at[k, A0], y_relay.at[0, dx], up)
            far_down[dx] = link(own.at[k, A1], y_relay.at[1, dx], down)
        if dy == 1:
            free_up[dx] = link(own.at[k, A1], y_in.at[0, dx, A1], up)
        if dy == 3:
            free_down[dx] = link(own.at[k, A0], y_in.at[1, dx, A0], down)

    def relay_rows(dx):
        far_up[dx].wait_recv()
        add(2 + dx, A0, y_relay[0, dx])
        near_up[dx] = link(own.at[2 + dx, A0], y_in.at[0, dx, A0], up)
        far_down[dx].wait_recv()
        add(6 + dx, A1, y_relay[1, dx])
        near_down[dx] = link(own.at[6 + dx, A1], y_in.at[1, dx, A1], down)

    relay_rows(1)
    x_first[2].wait_recv()
    add(4, B, x_in[2])
    late_far_up = link(own.at[4, B0], late_relay.at[0], up)
    late_far_down = link(own.at[4, B1], late_relay.at[1], down)
    relay_rows(0)
    x_first[1].wait_recv()
    add(2, B, x_in[1])
    late_free_up = link(own.at[2, B1], y_late.at[0, LATE1], up)
    x_first[3].wait_recv()
    add(6, B, x_in[3])
    late_free_down = link(own.at[6, B0], y_late.at[1, LATE0], down)
    for group in (free_up, near_up, free_down, near_down):
        group[1].wait_recv()
    own[1, A] = (
        own[1, A].astype(F32) + (y_in[0, 1].astype(F32) + y_in[1, 1].astype(F32))
    ).astype(BF)
    x_second = link(own.at[1, A], x_late, beside)
    late_far_up.wait_recv()
    add(2, B0, late_relay[0])
    late_near_up = link(own.at[2, B0], y_late.at[0, LATE0], up)
    late_far_down.wait_recv()
    add(6, B1, late_relay[1])
    late_near_down = link(own.at[6, B1], y_late.at[1, LATE1], down)
    each(REPLICAS, lambda step: left_late(step).start())
    each(REPLICAS, lambda step: right_copy(step).start())
    for group in (free_up, near_up, free_down, near_down):
        group[0].wait_recv()
    x_first[0].wait_recv()
    x_second.wait_recv()
    mean_y = (
        (own[0, A].astype(F32) + x_late[...].astype(F32))
        + (y_in[0, 0].astype(F32) + y_in[1, 0].astype(F32))
    ) * (1.0 / REPLICAS)
    grad_low[A] = mean_y.astype(BF)
    for copy in (late_free_up, late_near_up, late_free_down, late_near_down):
        copy.wait_recv()
    mean_x = (
        (own[0, B].astype(F32) + x_in[0].astype(F32))
        + (y_late[0].astype(F32) + y_late[1].astype(F32))
    ) * (1.0 / REPLICAS)
    grad_low[B] = mean_x.astype(BF)
    squares = jnp.sum((mean_x * mean_x).reshape(B_ROWS // 8, 8, SIDE), axis=0) + jnp.sum(
        (mean_y * mean_y).reshape(A_ROWS // 8, 8, SIDE), axis=0
    )
    tile2[0] = (squares[:, :128] + squares[:, 128:256]) + (squares[:, 256:384] + squares[:, 384:])

    def ring_copy(step):
        return remote(
            tile.at[0],
            tile.at[step],
            ring_send.at[step],
            ring_recv.at[step],
            dp=(me + step) % REPLICAS,
        )

    def column_copy(step):
        return remote(
            tile2.at[0],
            tile2.at[step],
            column_send.at[step],
            column_recv.at[step],
            fsdp=(column + step) % COLUMNS,
        )

    each(COLUMNS, lambda step: column_copy(step).start())
    each(REPLICAS, lambda step: right_late(step).start())
    for load in state_loads:
        load.wait()
    left_in[me] = left_basis[me]
    right_in[me] = right_basis[me]
    left_start = left_basis[...].reshape(SIDE, SIDE)
    right_start = right_basis[...].reshape(SIDE, SIDE)
    half_left = tn(left_start, grad_low[...]).astype(BF)
    rotated[...] = nn(half_left, right_start)
    each(COLUMNS, lambda step: column_copy(step).wait_recv())
    tile[0] = jnp.sum(tile2[...], axis=0)
    each(REPLICAS, lambda step: ring_copy(step).start())
    for copy in (left_copy, left_late):
        each(REPLICAS, lambda step, copy=copy: copy(step).wait_recv())
    send_rolled(left_in, left_rolled, left_moved, left_copy2)
    left_iter[...] = nt(grad_low[...], grad_low[...])
    right_iter[...] = tn(grad_low[...], grad_low[...])
    for copy in (right_copy, right_late):
        each(REPLICAS, lambda step, copy=copy: copy(step).wait_recv())
    send_rolled(right_in, right_rolled, right_moved, right_copy2)
    each(REPLICAS, lambda step: ring_copy(step).wait_recv())
    square_sum = jnp.sum(jnp.sum(tile[...], axis=0))
    entries = SIDE * SIDE * REPLICAS * COLUMNS
    clip_factor = jnp.minimum(1.0, CLIP_RMS * math.sqrt(entries) / jnp.sqrt(square_sum + 1e-06))

    weight = (1.0 - BETA_FACTOR) * (clip_factor * clip_factor)
    turned = clip_factor * rotated[...]
    moment = BETA_MOMENT * first_old[...].astype(F32) + (1.0 - BETA_MOMENT) * turned
    wide[:, 2 * CHUNK : 3 * CHUNK] = chunked(moment.astype(BF))
    left_new = (BETA_FACTOR * left_old[...] + weight * left_iter[...]).astype(BF)
    right_new = (BETA_FACTOR * right_old[...] + weight * right_iter[...]).astype(BF)
    wide[:, 0:CHUNK] = chunked(left_new)
    wide[:, CHUNK : 2 * CHUNK] = chunked(right_new)
    each(REPLICAS, lambda step: wide_copy(step).start())
    wide_in[me] = wide[me]
    second_new = BETA_SECOND * second_old[...] + (1.0 - BETA_SECOND) * turned * turned
    second[...] = chunked(second_new.astype(BF))
    second_in[me] = second[me]
    direction = (moment / (jnp.sqrt(second_new) + TINY)).astype(BF)
    half_back = nn(left_basis[...].reshape(SIDE, SIDE), direction).astype(BF)
    update = nt(half_back, right_basis[...].reshape(SIDE, SIDE))
    params_out[me] = (param_old[...].astype(F32) - STEP_RATE * update).astype(BF)

    far = index_of(y + 2, x, core)
    beside_down = index_of(y - 1, x + 1, core)
    beside_up = index_of(y + 1, x + 1, core)
    beside_far = index_of(y + 2, x + 1, core)
    copies, twins = [], []

    def pass_on(owner, rows, target):
        k = len(copies)
        view = params_out.at[owner, rows]
        copy = remote(view, view, ag_send.at[k], ag_recv.at[k], dp=target)
        copy.start()
        copies.append(copy)
        return copy

    def to_twin(owner, rows):
        k = len(twins)
        view = params_out.at[owner, rows]
        copy = remote(view, view, twin_send.at[k], twin_recv.at[k], dp=other)
        copy.start()
        twins.append(copy)

    x_own = pass_on(me, A, beside)
    b_up = pass_on(me, B, up)
    b_down = pass_on(me, B, down)
    a_up = pass_on(me, A, up)
    a_down = pass_on(me, A, down)
    x_same = pass_on(me, B, beside)
    to_twin(me, pl.ds(0, SIDE))

    def gather_second():
        x_own.wait_recv()
        steps = [pass_on(beside, A, up), pass_on(beside, A, down)]
        to_twin(beside, A)
        b_up.wait_recv()
        steps += [pass_on(down, B0, up), pass_on(down, B, beside)]
        to_twin(down, B)
        b_down.wait_recv()
        steps += [pass_on(up, B1, down), pass_on(up, B, beside)]
        to_twin(up, B)
        a_up.wait_recv()
        steps += [pass_on(down, A0, up)]
        to_twin(down, A)
        a_down.wait_recv()
        steps += [pass_on(up, A1, down)]
        to_twin(up, A)
        x_same.wait_recv()
        to_twin(beside, B)
        return steps

    def gather_third(steps):
        beside_a_up, beside_a_down, b_far0, b_x_down, b_far1, b_x_up, a_far0, a_far1 = steps
        b_far0.wait_recv()
        b_x_far0 = pass_on(far, B0, beside)
        to_twin(far, B0)
        b_far1.wait_recv()
        b_x_far1 = pass_on(far, B1, beside)
        to_twin(far, B1)
        beside_a_up.wait_recv()
        beside_far0 = pass_on(beside_down, A0, up)
        to_twin(beside_down, A)
        beside_a_down.wait_recv()
        beside_far1 = pass_on(beside_up, A1, down)
        to_twin(beside_up, A)
        a_far0.wait_recv()
        to_twin(far, A0)
        a_far1.wait_recv()
        to_twin(far, A1)
        b_x_down.wait_recv()
        to_twin(beside_down, B)
        b_x_up.wait_recv()
        to_twin(beside_up, B)
        return b_x_far0, b_x_far1, beside_far0, beside_far1

    def gather_last(steps):
        for copy, rows in zip(steps, (B0, B1, A0, A1)):
            copy.wait_recv()
            to_twin(beside_far, rows)

    each(REPLICAS, lambda step: wide_copy(step).wait_recv())
    send_rolled(wide_in, wide_rolled, wide_out, wide_copy2)
    second_steps = gather_second()
    each(REPLICAS, lambda step: second_copy(step).start())

    for copy in (left_copy2, right_copy2, wide_copy2):
        each(REPLICAS, lambda step, copy=copy: copy(step).wait_recv())
    left_start = left_moved[...].reshape(SIDE, SIDE)
    right_start = right_moved[...].reshape(SIDE, SIDE)
    for repeat in range(ITERS):
        image_step(
            wide_out[:, 0:CHUNK].reshape(SIDE, SIDE),
            left_start if repeat == 0 else left_low[...],
            left_iter,
            left_low,
        )
        image_step(
            wide_out[:, CHUNK : 2 * CHUNK].reshape(SIDE, SIDE),
            right_start if repeat == 0 else right_low[...],
            right_iter,
            right_low,
        )
        for newton in range(NEWTON):
            newton_step(left_iter, left_low, left_gram)
            newton_step(right_iter, right_low, right_gram)
    left_turn = tn(left_low[...], left_start).astype(BF)
    right_turn = tn(right_start, right_low[...]).astype(BF)
    moment_low = wide_out[:, 2 * CHUNK : 3 * CHUNK].reshape(SIDE, SIDE)
    half_turned = nn(left_turn, moment_low).astype(BF)
    first_out[...] = nn(half_turned, right_turn).astype(BF)

    last_steps = gather_third(second_steps)
    each(REPLICAS, lambda step: second_copy(step).wait_recv())
    send_rolled(second_in, second_rolled, second_out, second_copy2)
    gather_last(last_steps)

    for copy in swaps.values():
        copy.wait_send()
    for copy in links:
        copy.wait_send()
    each(REPLICAS, lambda step: ring_copy(step).wait_send())
    each(COLUMNS, lambda step: column_copy(step).wait_send())
    for copy in twins:
        copy.wait()
    for copy in copies:
        copy.wait_send()
    early = (left_copy, left_late, right_copy, right_late, left_copy2, right_copy2)
    for copy in early + (wide_copy, second_copy, wide_copy2):
        each(REPLICAS, lambda step, copy=copy: copy(step).wait_send())
    each(REPLICAS, lambda step: second_copy2(step).wait())


def step(arrays, rotation):
    hbm = pl.BlockSpec(memory_space=pl.ANY)
    dma = pltpu.SemaphoreType.DMA
    slots = (REPLICAS, CHUNK, SIDE)
    moved = (REPLICAS, 3 * CHUNK, SIDE)

    def block(dtype):
        return pltpu.VMEM((SIDE, SIDE), dtype)

    arrays = [pltpu.with_memory_space_constraint(array, pltpu.HBM) for array in arrays]
    return pl.pallas_call(
        step_kernel,
        out_shape=(
            pltpu.VMEM((REPLICAS, SIDE, SIDE), BF),
            pltpu.VMEM(moved, BF),
            pltpu.VMEM(slots, BF),
            block(BF),
            block(BF),
            block(BF),
        ),
        in_specs=[hbm] * len(arrays) + [pl.BlockSpec(memory_space=pltpu.SMEM)],
        out_specs=(pl.BlockSpec(memory_space=pltpu.VMEM),) * 6,
        scratch_shapes=[
            pltpu.VMEM((8, SIDE, SIDE), BF),
            pltpu.VMEM((8, SIDE, SIDE), BF),
            pltpu.VMEM((4, B_ROWS, SIDE), BF),
            pltpu.VMEM((2, 2, A_HALF, SIDE), BF),
            pltpu.VMEM((2, 2, A_ROWS, SIDE), BF),
            pltpu.VMEM((2, B_HALF, SIDE), BF),
            pltpu.VMEM((2, B_ROWS, SIDE), BF),
            pltpu.VMEM((A_ROWS, SIDE), BF),
            pltpu.VMEM((REPLICAS, 8, 128), F32),
            pltpu.VMEM((COLUMNS, 8, 128), F32),
            block(F32),
            block(F32),
            block(F32),
            pltpu.VMEM(slots, BF),
            pltpu.VMEM(slots, BF),
            block(BF),
            block(BF),
            block(BF),
            block(F32),
            block(F32),
            block(F32),
            block(BF),
            block(BF),
        ]
        + [pltpu.VMEM(moved, BF)] * 3
        + [pltpu.VMEM(slots, BF)] * 9
        + [dma((8,)), dma((7,)), dma((8,)), dma((8,)), dma((23,)), dma((23,))]
        + [dma((REPLICAS,))] * 2
        + [dma((COLUMNS,))] * 2
        + [dma((18,))] * 2
        + [dma((19,))] * 2
        + [dma((REPLICAS,))] * 20,
        compiler_params=pltpu.CompilerParams(
            collective_id=0, has_side_effects=True, vmem_limit_bytes=46 * 2**20
        ),
        cost_estimate=pl.CostEstimate(
            flops=10**10, bytes_accessed=32 * 2**20, transcendentals=0
        ),
        name="soap_step",
    )(*arrays, rotation)


def finish_kernel(
    params,
    wide,
    second,
    left_low,
    right_low,
    first,
    params_out,
    left_out,
    right_out,
    second_out,
    left_basis_out,
    right_basis_out,
    first_out,
    staged,
    sems,
):
    copies = [
        pltpu.make_async_copy(source, target, sems.at[k])
        for k, (source, target) in enumerate(
            (
                *(
                    (params.at[pl.ds(4 * part, 4)], params_out.at[pl.ds(4 * part, 4)])
                    for part in range(4)
                ),
                (left_low, left_basis_out),
                (right_low, right_basis_out),
                (first, first_out),
            )
        )
    ]
    for copy in copies:
        copy.start()
    for k, target in enumerate((left_out, right_out, second_out)):
        source = second[...] if k == 2 else wide[:, CHUNK * k : CHUNK * (k + 1)]
        staged[k] = source.astype(F32)
        copies.append(pltpu.make_async_copy(staged.at[k], target, sems.at[7 + k]))
        copies[-1].start()
    for copy in copies:
        copy.wait()


def finish(arrays):
    slots = (REPLICAS, CHUNK, SIDE)
    return pl.pallas_call(
        finish_kernel,
        out_shape=(pltpu.HBM((REPLICAS, SIDE, SIDE), BF),)
        + (pltpu.HBM(slots, F32),) * 3
        + (pltpu.HBM((SIDE, SIDE), BF),) * 3,
        in_specs=[pl.BlockSpec(memory_space=pltpu.VMEM)] * len(arrays),
        out_specs=(pl.BlockSpec(memory_space=pl.ANY),) * 7,
        scratch_shapes=[
            pltpu.VMEM((3,) + slots, F32),
            pltpu.SemaphoreType.DMA((10,)),
        ],
        compiler_params=pltpu.CompilerParams(vmem_limit_bytes=24 * 2**20),
        cost_estimate=pl.CostEstimate(flops=0, bytes_accessed=24 * 2**20, transcendentals=0),
        name="finish",
    )(*arrays)


def local(
    grads,
    left_factor,
    right_factor,
    left_basis,
    right_basis,
    first_moment,
    second_moment,
    parameters,
    rotation,
):
    blocks = (
        left_factor,
        right_factor,
        second_moment,
        left_basis,
        right_basis,
        first_moment,
        parameters,
    )
    slots = (REPLICAS, CHUNK, SIDE)
    arrays = [grads[0, :, 0]] + [value[0, 0] for value in blocks]
    for k in (4, 5):
        arrays[k] = arrays[k].reshape(slots)
    gathered, *outs = finish(step(arrays, rotation))
    left, right, second, left_turned, right_turned, first = (
        value.reshape(1, 1, SIDE, SIDE) for value in outs
    )
    return (gathered[:, None], left, right, left_turned, right_turned, first, second)


def solution(mesh):
    state = P("dp", "fsdp", None, None)
    return jax.shard_map(
        local,
        mesh=mesh,
        in_specs=(P("dp", None, "fsdp", None, None),) + (state,) * 7 + (P("fsdp"),),
        out_specs=(P(None, "fsdp", None, None),) + (state,) * 6,
        check_vma=False,
    )
```

```python
import math

import jax
import jax.numpy as jnp
from jax import lax
from jax.experimental import pallas as pl
from jax.experimental.pallas import tpu as pltpu
from jax.sharding import PartitionSpec as P

ITERS = 2
NEWTON = 3
SIDE = 512
REPLICAS = 16
COLUMNS = 8
CHUNK = SIDE // REPLICAS

BETA_MOMENT = 0.95
BETA_SECOND = 0.95
BETA_FACTOR = 0.95
STEP_RATE = 0.05
CLIP_RMS = 0.3
TINY = 1e-08

A_HALF = 144
A_ROWS = 2 * A_HALF
B_ROWS = SIDE - A_ROWS
B_HALF = B_ROWS // 2
A = pl.ds(0, A_ROWS)
B = pl.ds(A_ROWS, B_ROWS)
A0, A1 = pl.ds(0, A_HALF), pl.ds(A_HALF, A_HALF)
B0, B1 = pl.ds(A_ROWS, B_HALF), pl.ds(A_ROWS + B_HALF, B_HALF)
LATE0, LATE1 = pl.ds(0, B_HALF), pl.ds(B_HALF, B_HALF)

MESH = pl.DeviceIdType.MESH
BF = jnp.bfloat16
F32 = jnp.float32


def place():
    me = lax.axis_index("dp")
    return me, me // 4, me // 2 % 2, me % 2


def index_of(y, x, core):
    return y % 4 * 4 + x % 2 * 2 + core % 2


def remote(src, dst, send, recv, **where):
    return pltpu.make_async_remote_copy(
        src_ref=src, dst_ref=dst, send_sem=send, recv_sem=recv, device_id=where, device_id_type=MESH
    )


def greet_replicas(barrier, me):
    def greet(step, carry):
        pl.semaphore_signal(
            barrier, inc=1, device_id={"dp": (me + step) % REPLICAS}, device_id_type=MESH
        )
        return carry

    lax.fori_loop(1, REPLICAS, greet, 0)


def nn(a, b):
    return jnp.dot(a, b, preferred_element_type=F32)


def nt(a, b):
    return lax.dot_general(a, b, (((1,), (1,)), ((), ())), preferred_element_type=F32)


def tn(a, b):
    return lax.dot_general(a, b, (((0,), (0,)), ((), ())), preferred_element_type=F32)


def each(count, act):
    lax.fori_loop(1, count, lambda step, carry: (act(step), carry)[1], 0)


def chunked(value):
    return value.reshape(REPLICAS, CHUNK, SIDE)


def image_step(factor, basis, iterate, low):
    image = nn(factor, basis)
    magnitude = jnp.abs(image)
    bound = (
        jnp.sqrt(jnp.max(jnp.sum(magnitude, axis=0)) * jnp.max(jnp.sum(magnitude, axis=1)))
        + 1e-06
    )
    scaled = image * (1.0 / bound)
    iterate[...] = scaled
    low[...] = scaled.astype(BF)


def newton_step(iterate, low, gram):
    gram[...] = nt(low[...], low[...]).astype(BF)
    value = 1.5 * iterate[...] - 0.5 * nn(gram[...], low[...])
    iterate[...] = value
    low[...] = value.astype(BF)


def step_kernel(
    grads,
    left_hbm,
    right_hbm,
    second_hbm,
    left_basis_hbm,
    right_basis_hbm,
    first_hbm,
    param_hbm,
    rotation,
    params_out,
    wide_out,
    second_out,
    left_low,
    right_low,
    first_out,
    own,
    twin,
    x_in,
    y_relay,
    y_in,
    late_relay,
    y_late,
    x_late,
    tile,
    tile2,
    left_old,
    right_old,
    second_old,
    left_basis,
    right_basis,
    first_old,
    param_old,
    grad_low,
    rotated,
    left_iter,
    right_iter,
    left_gram,
    right_gram,
    wide,
    wide_in,
    wide_rolled,
    left_in,
    left_rolled,
    left_moved,
    right_in,
    right_rolled,
    right_moved,
    second,
    second_in,
    second_rolled,
    local_sem,
    load_sem,
    core_send,
    core_recv,
    send,
    recv,
    ring_send,
    ring_recv,
    column_send,
    column_recv,
    ag_send,
    ag_recv,
    twin_send,
    twin_recv,
    wide_send,
    wide_recv,
    wide_send2,
    wide_recv2,
    second_send,
    second_recv,
    second_send2,
    second_recv2,
    left_late_send,
    left_late_recv,
    left_send,
    left_recv,
    left_send2,
    left_recv2,
    right_late_send,
    right_late_recv,
    right_send,
    right_recv,
    right_send2,
    right_recv2,
):
    me, y, x, core = place()
    column = lax.axis_index("fsdp")
    barrier = pltpu.get_barrier_semaphore()
    greet_replicas(barrier, me)
    z, x_high = column // 2, column % 2

    def greet(dp, fsdp):
        pl.semaphore_signal(
            barrier, inc=1, device_id={"dp": dp, "fsdp": fsdp}, device_id_type=MESH
        )

    def greet_plane(step, carry):
        greet(index_of(y + step // 2, x + step, core), z * 2 + (1 - x_high))
        return carry

    def greet_line(step, carry):
        greet(index_of(y, x, core + step), (z + step // 2) % 4 * 2 + x_high)
        return carry

    lax.fori_loop(0, 8, greet_plane, 0)
    lax.fori_loop(2, 8, greet_line, 0)

    beside = index_of(y, x + 1, core)
    other = index_of(y, x, core + 1)
    up = index_of(y + 1, x, core)
    down = index_of(y - 1, x, core)
    order = [(2, 1), (2, 0), (1, 1), (3, 1), (1, 0), (3, 0), (0, 1), (0, 0)]
    loads, swaps = {}, {}
    for dy, dx in order:
        k = dy * 2 + dx
        loads[dy, dx] = pltpu.make_async_copy(
            grads.at[index_of(y + dy, x + dx, core)], own.at[k], local_sem.at[k]
        )
        loads[dy, dx].start()
    pl.semaphore_wait(barrier, REPLICAS - 1 + 14)
    for dy, dx in order:
        k = dy * 2 + dx
        swaps[dy, dx] = remote(
            grads.at[index_of(y + dy, x + dx, core + 1)],
            twin.at[k],
            core_send.at[k],
            core_recv.at[k],
            dp=other,
        )
        swaps[dy, dx].start()

    state_loads = [
        pltpu.make_async_copy(source, target, load_sem.at[k])
        for k, (source, target) in enumerate(
            (
                (left_basis_hbm, left_basis),
                (right_basis_hbm, right_basis),
                (first_hbm, first_old),
                (second_hbm, second_old),
                (left_hbm, left_old),
                (right_hbm, right_old),
                (param_hbm, param_old),
            )
        )
    ]
    for load in state_loads:
        load.start()

    shift = rotation[0]

    def state_copy(source, target, sends, recvs, step):
        there = (me + step) % REPLICAS
        return remote(
            source.at[there], target.at[me], sends.at[step], recvs.at[step], dp=there
        )

    def send_rolled(source, rolled, target, copy):
        def one(step):
            there = (me + step) % REPLICAS
            rolled[there] = source[(there + REPLICAS - shift) % REPLICAS]
            copy(step).start()

        each(REPLICAS, one)
        target[me] = source[(me + REPLICAS - shift) % REPLICAS]

    def half_copy(source, target, start, sends, recvs, step):
        there = (me + step) % REPLICAS
        rows = pl.ds(start, CHUNK // 2)
        return remote(
            source.at[there, rows], target.at[me, rows], sends.at[step], recvs.at[step], dp=there
        )

    def left_copy(step):
        return half_copy(left_basis_hbm, left_in, 0, left_send, left_recv, step)

    def left_late(step):
        return half_copy(
            left_basis_hbm, left_in, CHUNK // 2, left_late_send, left_late_recv, step
        )

    def left_copy2(step):
        return state_copy(left_rolled, left_moved, left_send2, left_recv2, step)

    def right_copy(step):
        return half_copy(right_basis_hbm, right_in, 0, right_send, right_recv, step)

    def right_late(step):
        return half_copy(
            right_basis_hbm, right_in, CHUNK // 2, right_late_send, right_late_recv, step
        )

    def right_copy2(step):
        return state_copy(right_rolled, right_moved, right_send2, right_recv2, step)

    def wide_copy(step):
        return state_copy(wide, wide_in, wide_send, wide_recv, step)

    def wide_copy2(step):
        return state_copy(wide_rolled, wide_out, wide_send2, wide_recv2, step)

    def second_copy(step):
        return state_copy(second, second_in, second_send, second_recv, step)

    def second_copy2(step):
        return state_copy(second_rolled, second_out, second_send2, second_recv2, step)

    each(REPLICAS, lambda step: left_copy(step).start())

    links = []

    def link(source, target, device):
        k = len(links)
        copy = remote(source, target, send.at[k], recv.at[k], dp=device)
        copy.start()
        links.append(copy)
        return copy

    def add(k, rows, value):
        own[k, rows] = own[k, rows] + value

    x_first, far_up, far_down, free_up, free_down, near_up, near_down = ({} for _ in range(7))
    for dy, dx in order:
        k = dy * 2 + dx
        loads[dy, dx].wait()
        swaps[dy, dx].wait_recv()
        own[k] = own[k] + twin[k]
        if dx == 1:
            x_first[dy] = link(own.at[k, B], x_in.at[dy], beside)
        if dy == 2:
            far_up[dx] = link(own.at[k, A0], y_relay.at[0, dx], up)
            far_down[dx] = link(own.at[k, A1], y_relay.at[1, dx], down)
        if dy == 1:
            free_up[dx] = link(own.at[k, A1], y_in.at[0, dx, A1], up)
        if dy == 3:
            free_down[dx] = link(own.at[k, A0], y_in.at[1, dx, A0], down)

    def relay_rows(dx):
        far_up[dx].wait_recv()
        add(2 + dx, A0, y_relay[0, dx])
        near_up[dx] = link(own.at[2 + dx, A0], y_in.at[0, dx, A0], up)
        far_down[dx].wait_recv()
        add(6 + dx, A1, y_relay[1, dx])
        near_down[dx] = link(own.at[6 + dx, A1], y_in.at[1, dx, A1], down)

    relay_rows(1)
    x_first[2].wait_recv()
    add(4, B, x_in[2])
    late_far_up = link(own.at[4, B0], late_relay.at[0], up)
    late_far_down = link(own.at[4, B1], late_relay.at[1], down)
    relay_rows(0)
    x_first[1].wait_recv()
    add(2, B, x_in[1])
    late_free_up = link(own.at[2, B1], y_late.at[0, LATE1], up)
    x_first[3].wait_recv()
    add(6, B, x_in[3])
    late_free_down = link(own.at[6, B0], y_late.at[1, LATE0], down)
    for group in (free_up, near_up, free_down, near_down):
        group[1].wait_recv()
    own[1, A] = (
        own[1, A].astype(F32) + (y_in[0, 1].astype(F32) + y_in[1, 1].astype(F32))
    ).astype(BF)
    x_second = link(own.at[1, A], x_late, beside)
    late_far_up.wait_recv()
    add(2, B0, late_relay[0])
    late_near_up = link(own.at[2, B0], y_late.at[0, LATE0], up)
    late_far_down.wait_recv()
    add(6, B1, late_relay[1])
    late_near_down = link(own.at[6, B1], y_late.at[1, LATE1], down)
    each(REPLICAS, lambda step: left_late(step).start())
    each(REPLICAS, lambda step: right_copy(step).start())
    for group in (free_up, near_up, free_down, near_down):
        group[0].wait_recv()
    x_first[0].wait_recv()
    x_second.wait_recv()
    mean_y = (
        (own[0, A].astype(F32) + x_late[...].astype(F32))
        + (y_in[0, 0].astype(F32) + y_in[1, 0].astype(F32))
    ) * (1.0 / REPLICAS)
    grad_low[A] = mean_y.astype(BF)
    for copy in (late_free_up, late_near_up, late_free_down, late_near_down):
        copy.wait_recv()
    mean_x = (
        (own[0, B].astype(F32) + x_in[0].astype(F32))
        + (y_late[0].astype(F32) + y_late[1].astype(F32))
    ) * (1.0 / REPLICAS)
    grad_low[B] = mean_x.astype(BF)
    squares = jnp.sum((mean_x * mean_x).reshape(B_ROWS // 8, 8, SIDE), axis=0) + jnp.sum(
        (mean_y * mean_y).reshape(A_ROWS // 8, 8, SIDE), axis=0
    )
    tile2[0] = (squares[:, :128] + squares[:, 128:256]) + (squares[:, 256:384] + squares[:, 384:])

    def column_copy(step):
        there = (z * 2 + core + step) % COLUMNS
        return remote(
            tile2.at[0],
            tile2.at[step],
            column_send.at[step],
            column_recv.at[step],
            dp=index_of(y, x, there % 2),
            fsdp=there // 2 * 2 + x_high,
        )

    def ring_copy(step):
        there = (y * 4 + x * 2 + x_high + step) % REPLICAS
        return remote(
            tile.at[0],
            tile.at[step],
            ring_send.at[step],
            ring_recv.at[step],
            dp=index_of(there // 4, there // 2, core),
            fsdp=z * 2 + there % 2,
        )

    each(COLUMNS, lambda step: column_copy(step).start())
    each(REPLICAS, lambda step: right_late(step).start())
    for load in state_loads:
        load.wait()
    left_in[me] = left_basis[me]
    right_in[me] = right_basis[me]
    left_start = left_basis[...].reshape(SIDE, SIDE)
    right_start = right_basis[...].reshape(SIDE, SIDE)
    half_left = tn(left_start, grad_low[...]).astype(BF)
    rotated[...] = nn(half_left, right_start)
    each(COLUMNS, lambda step: column_copy(step).wait_recv())
    tile[0] = jnp.sum(tile2[...], axis=0)
    each(REPLICAS, lambda step: ring_copy(step).start())
    for copy in (left_copy, left_late):
        each(REPLICAS, lambda step, copy=copy: copy(step).wait_recv())
    send_rolled(left_in, left_rolled, left_moved, left_copy2)
    left_iter[...] = nt(grad_low[...], grad_low[...])
    right_iter[...] = tn(grad_low[...], grad_low[...])
    for copy in (right_copy, right_late):
        each(REPLICAS, lambda step, copy=copy: copy(step).wait_recv())
    send_rolled(right_in, right_rolled, right_moved, right_copy2)
    each(REPLICAS, lambda step: ring_copy(step).wait_recv())
    square_sum = jnp.sum(jnp.sum(tile[...], axis=0))
    entries = SIDE * SIDE * REPLICAS * COLUMNS
    clip_factor = jnp.minimum(1.0, CLIP_RMS * math.sqrt(entries) / jnp.sqrt(square_sum + 1e-06))

    weight = (1.0 - BETA_FACTOR) * (clip_factor * clip_factor)
    turned = clip_factor * rotated[...]
    moment = BETA_MOMENT * first_old[...].astype(F32) + (1.0 - BETA_MOMENT) * turned
    wide[:, 2 * CHUNK : 3 * CHUNK] = chunked(moment.astype(BF))
    left_new = (BETA_FACTOR * left_old[...] + weight * left_iter[...]).astype(BF)
    right_new = (BETA_FACTOR * right_old[...] + weight * right_iter[...]).astype(BF)
    wide[:, 0:CHUNK] = chunked(left_new)
    wide[:, CHUNK : 2 * CHUNK] = chunked(right_new)
    each(REPLICAS, lambda step: wide_copy(step).start())
    wide_in[me] = wide[me]
    second_new = BETA_SECOND * second_old[...] + (1.0 - BETA_SECOND) * turned * turned
    second[...] = chunked(second_new.astype(BF))
    second_in[me] = second[me]
    direction = (moment / (jnp.sqrt(second_new) + TINY)).astype(BF)
    half_back = nn(left_basis[...].reshape(SIDE, SIDE), direction).astype(BF)
    update = nt(half_back, right_basis[...].reshape(SIDE, SIDE))
    params_out[me] = (param_old[...].astype(F32) - STEP_RATE * update).astype(BF)

    far = index_of(y + 2, x, core)
    beside_down = index_of(y - 1, x + 1, core)
    beside_up = index_of(y + 1, x + 1, core)
    beside_far = index_of(y + 2, x + 1, core)
    copies, twins = [], []

    def pass_on(owner, rows, target):
        k = len(copies)
        view = params_out.at[owner, rows]
        copy = remote(view, view, ag_send.at[k], ag_recv.at[k], dp=target)
        copy.start()
        copies.append(copy)
        return copy

    def to_twin(owner, rows):
        k = len(twins)
        view = params_out.at[owner, rows]
        copy = remote(view, view, twin_send.at[k], twin_recv.at[k], dp=other)
        copy.start()
        twins.append(copy)

    x_own = pass_on(me, A, beside)
    b_up = pass_on(me, B, up)
    b_down = pass_on(me, B, down)
    a_up = pass_on(me, A, up)
    a_down = pass_on(me, A, down)
    x_same = pass_on(me, B, beside)
    to_twin(me, pl.ds(0, SIDE))

    def gather_second():
        x_own.wait_recv()
        steps = [pass_on(beside, A, up), pass_on(beside, A, down)]
        to_twin(beside, A)
        b_up.wait_recv()
        steps += [pass_on(down, B0, up), pass_on(down, B, beside)]
        to_twin(down, B)
        b_down.wait_recv()
        steps += [pass_on(up, B1, down), pass_on(up, B, beside)]
        to_twin(up, B)
        a_up.wait_recv()
        steps += [pass_on(down, A0, up)]
        to_twin(down, A)
        a_down.wait_recv()
        steps += [pass_on(up, A1, down)]
        to_twin(up, A)
        x_same.wait_recv()
        to_twin(beside, B)
        return steps

    def gather_third(steps):
        beside_a_up, beside_a_down, b_far0, b_x_down, b_far1, b_x_up, a_far0, a_far1 = steps
        b_far0.wait_recv()
        b_x_far0 = pass_on(far, B0, beside)
        to_twin(far, B0)
        b_far1.wait_recv()
        b_x_far1 = pass_on(far, B1, beside)
        to_twin(far, B1)
        beside_a_up.wait_recv()
        beside_far0 = pass_on(beside_down, A0, up)
        to_twin(beside_down, A)
        beside_a_down.wait_recv()
        beside_far1 = pass_on(beside_up, A1, down)
        to_twin(beside_up, A)
        a_far0.wait_recv()
        to_twin(far, A0)
        a_far1.wait_recv()
        to_twin(far, A1)
        b_x_down.wait_recv()
        to_twin(beside_down, B)
        b_x_up.wait_recv()
        to_twin(beside_up, B)
        return b_x_far0, b_x_far1, beside_far0, beside_far1

    def gather_last(steps):
        for copy, rows in zip(steps, (B0, B1, A0, A1)):
            copy.wait_recv()
            to_twin(beside_far, rows)

    each(REPLICAS, lambda step: wide_copy(step).wait_recv())
    send_rolled(wide_in, wide_rolled, wide_out, wide_copy2)
    second_steps = gather_second()
    each(REPLICAS, lambda step: second_copy(step).start())

    for copy in (left_copy2, right_copy2, wide_copy2):
        each(REPLICAS, lambda step, copy=copy: copy(step).wait_recv())
    left_start = left_moved[...].reshape(SIDE, SIDE)
    right_start = right_moved[...].reshape(SIDE, SIDE)
    for repeat in range(ITERS):
        image_step(
            wide_out[:, 0:CHUNK].reshape(SIDE, SIDE),
            left_start if repeat == 0 else left_low[...],
            left_iter,
            left_low,
        )
        image_step(
            wide_out[:, CHUNK : 2 * CHUNK].reshape(SIDE, SIDE),
            right_start if repeat == 0 else right_low[...],
            right_iter,
            right_low,
        )
        for newton in range(NEWTON):
            newton_step(left_iter, left_low, left_gram)
            newton_step(right_iter, right_low, right_gram)
    left_turn = tn(left_low[...], left_start).astype(BF)
    right_turn = tn(right_start, right_low[...]).astype(BF)
    moment_low = wide_out[:, 2 * CHUNK : 3 * CHUNK].reshape(SIDE, SIDE)
    half_turned = nn(left_turn, moment_low).astype(BF)
    first_out[...] = nn(half_turned, right_turn).astype(BF)

    last_steps = gather_third(second_steps)
    each(REPLICAS, lambda step: second_copy(step).wait_recv())
    send_rolled(second_in, second_rolled, second_out, second_copy2)
    gather_last(last_steps)

    for copy in swaps.values():
        copy.wait_send()
    for copy in links:
        copy.wait_send()
    each(REPLICAS, lambda step: ring_copy(step).wait_send())
    each(COLUMNS, lambda step: column_copy(step).wait_send())
    for copy in twins:
        copy.wait()
    for copy in copies:
        copy.wait_send()
    early = (left_copy, left_late, right_copy, right_late, left_copy2, right_copy2)
    for copy in early + (wide_copy, second_copy, wide_copy2):
        each(REPLICAS, lambda step, copy=copy: copy(step).wait_send())
    each(REPLICAS, lambda step: second_copy2(step).wait())


def step(arrays, rotation):
    hbm = pl.BlockSpec(memory_space=pl.ANY)
    dma = pltpu.SemaphoreType.DMA
    slots = (REPLICAS, CHUNK, SIDE)
    moved = (REPLICAS, 3 * CHUNK, SIDE)

    def block(dtype):
        return pltpu.VMEM((SIDE, SIDE), dtype)

    arrays = [pltpu.with_memory_space_constraint(array, pltpu.HBM) for array in arrays]
    return pl.pallas_call(
        step_kernel,
        out_shape=(
            pltpu.VMEM((REPLICAS, SIDE, SIDE), BF),
            pltpu.VMEM(moved, BF),
            pltpu.VMEM(slots, BF),
            block(BF),
            block(BF),
            block(BF),
        ),
        in_specs=[hbm] * len(arrays) + [pl.BlockSpec(memory_space=pltpu.SMEM)],
        out_specs=(pl.BlockSpec(memory_space=pltpu.VMEM),) * 6,
        scratch_shapes=[
            pltpu.VMEM((8, SIDE, SIDE), BF),
            pltpu.VMEM((8, SIDE, SIDE), BF),
            pltpu.VMEM((4, B_ROWS, SIDE), BF),
            pltpu.VMEM((2, 2, A_HALF, SIDE), BF),
            pltpu.VMEM((2, 2, A_ROWS, SIDE), BF),
            pltpu.VMEM((2, B_HALF, SIDE), BF),
            pltpu.VMEM((2, B_ROWS, SIDE), BF),
            pltpu.VMEM((A_ROWS, SIDE), BF),
            pltpu.VMEM((REPLICAS, 8, 128), F32),
            pltpu.VMEM((COLUMNS, 8, 128), F32),
            block(F32),
            block(F32),
            block(F32),
            pltpu.VMEM(slots, BF),
            pltpu.VMEM(slots, BF),
            block(BF),
            block(BF),
            block(BF),
            block(F32),
            block(F32),
            block(F32),
            block(BF),
            block(BF),
        ]
        + [pltpu.VMEM(moved, BF)] * 3
        + [pltpu.VMEM(slots, BF)] * 9
        + [dma((8,)), dma((7,)), dma((8,)), dma((8,)), dma((23,)), dma((23,))]
        + [dma((REPLICAS,))] * 2
        + [dma((COLUMNS,))] * 2
        + [dma((18,))] * 2
        + [dma((19,))] * 2
        + [dma((REPLICAS,))] * 20,
        compiler_params=pltpu.CompilerParams(
            collective_id=0, has_side_effects=True, vmem_limit_bytes=46 * 2**20
        ),
        cost_estimate=pl.CostEstimate(
            flops=10**10, bytes_accessed=32 * 2**20, transcendentals=0
        ),
        name="soap_step",
    )(*arrays, rotation)


def finish_kernel(
    params,
    wide,
    second,
    left_low,
    right_low,
    first,
    params_out,
    left_out,
    right_out,
    second_out,
    left_basis_out,
    right_basis_out,
    first_out,
    staged,
    sems,
):
    copies = [
        pltpu.make_async_copy(source, target, sems.at[k])
        for k, (source, target) in enumerate(
            (
                *(
                    (params.at[pl.ds(4 * part, 4)], params_out.at[pl.ds(4 * part, 4)])
                    for part in range(4)
                ),
                (left_low, left_basis_out),
                (right_low, right_basis_out),
                (first, first_out),
            )
        )
    ]
    for copy in copies:
        copy.start()
    for k, target in enumerate((left_out, right_out, second_out)):
        source = second[...] if k == 2 else wide[:, CHUNK * k : CHUNK * (k + 1)]
        staged[k] = source.astype(F32)
        copies.append(pltpu.make_async_copy(staged.at[k], target, sems.at[7 + k]))
        copies[-1].start()
    for copy in copies:
        copy.wait()


def finish(arrays):
    slots = (REPLICAS, CHUNK, SIDE)
    return pl.pallas_call(
        finish_kernel,
        out_shape=(pltpu.HBM((REPLICAS, SIDE, SIDE), BF),)
        + (pltpu.HBM(slots, F32),) * 3
        + (pltpu.HBM((SIDE, SIDE), BF),) * 3,
        in_specs=[pl.BlockSpec(memory_space=pltpu.VMEM)] * len(arrays),
        out_specs=(pl.BlockSpec(memory_space=pl.ANY),) * 7,
        scratch_shapes=[
            pltpu.VMEM((3,) + slots, F32),
            pltpu.SemaphoreType.DMA((10,)),
        ],
        compiler_params=pltpu.CompilerParams(vmem_limit_bytes=24 * 2**20),
        cost_estimate=pl.CostEstimate(flops=0, bytes_accessed=24 * 2**20, transcendentals=0),
        name="finish",
    )(*arrays)


def local(
    grads,
    left_factor,
    right_factor,
    left_basis,
    right_basis,
    first_moment,
    second_moment,
    parameters,
    rotation,
):
    blocks = (
        left_factor,
        right_factor,
        second_moment,
        left_basis,
        right_basis,
        first_moment,
        parameters,
    )
    slots = (REPLICAS, CHUNK, SIDE)
    arrays = [grads[0, :, 0]] + [value[0, 0] for value in blocks]
    for k in (4, 5):
        arrays[k] = arrays[k].reshape(slots)
    gathered, *outs = finish(step(arrays, rotation))
    left, right, second, left_turned, right_turned, first = (
        value.reshape(1, 1, SIDE, SIDE) for value in outs
    )
    return (gathered[:, None], left, right, left_turned, right_turned, first, second)


def solution(mesh):
    state = P("dp", "fsdp", None, None)
    return jax.shard_map(
        local,
        mesh=mesh,
        in_specs=(P("dp", None, "fsdp", None, None),) + (state,) * 7 + (P("fsdp"),),
        out_specs=(P(None, "fsdp", None, None),) + (state,) * 6,
        check_vma=False,
    )
```
